32 devices in a mesh: tm: 8 (over z, x), fiber: 4 (over y, core).
Axes of the slice: x: 2, y: 2, z: 4, core: 2. Of those that a mesh axis runs over, the one named last changes fastest.
Arguments:
- signal: float32 [128, 4096], P('fiber', 'tm'), may hold values from -6 to 6
- encode_weight: float32 [64, 9], replicated, may hold values from -2 to 2
- encode_bias: float32 [64], replicated, may hold values from -3 to 3
- dilated_weight: float32 [6, 6, 64, 64], replicated, may hold values from -0.3125 to 0.3125
- dilated_bias: float32 [6, 64], replicated, may hold values from -3 to 3
- decode_weight: float32 [9, 64], replicated, may hold values from -0.5 to 0.5
Outputs:
- recon: float32 [128, 4096], P('fiber', 'tm')
- tile_error: float32 [8, 32], P('fiber', 'tm')
The draws below stay inside these ranges and needn't reach their ends.
All inputs are finite; a program needn't handle non-finite values.
Results may differ from the reference program's by a relative error of at most 0.0001.
Values sent between devices are 32-bit elements; how exact they have to be, the bound alone decides.
No kernel may reach another device: no remote copies, remote signals or barrier semaphores. Data moves between devices by JAX's collectives and lax.ppermute only.
A program may use at most 64 MiB of HBM per device.

```python
import jax
import jax.numpy as jnp
from jax import lax

FEATURES = 64
LAYERS = 6
TILE_C = 16
TILE_T = 128
CH = 128
TM = 4096


def shard_levels(own_key, shape, split, low, top_value):
    factor_of = 1.0
    for dim, shards_of in split:
        heights = jax.random.uniform(jax.random.fold_in(jax.random.fold_in(own_key, 6), dim), (shards_of,), jnp.float32, low / len(split), top_value / len(split))
        factor_of = factor_of * jnp.repeat(jnp.exp(heights), shape[dim] // shards_of).reshape((-1,) + (1,) * (len(shape) - 1 - dim))
    return factor_of


def centred(stream_key, shape, scale, most, shards=(), held_as=jnp.bfloat16):
    loudness = shard_levels(stream_key, shape, shards, -0.22, 0.18) if shards else 1.0
    entries = jax.random.normal(stream_key, shape, jnp.float32) * scale * loudness
    return jnp.minimum(jnp.maximum(entries, -most), most).astype(held_as)


def setup_inputs(seed: int = 0) -> dict:
    arg_keys = jax.random.split(jax.random.key(seed), 7)
    signal = centred(arg_keys[0], (CH, TM), 1.0, 6.0, ((0, 4), (1, 8)), jnp.float32)
    encode_weight = centred(arg_keys[1], (FEATURES, 9), 9 ** -0.5, 2.0, (), jnp.float32)
    encode_bias = centred(arg_keys[2], (FEATURES,), 0.5, 3.0, (), jnp.float32)
    dilated_weight = centred(arg_keys[3], (LAYERS, 6, FEATURES, FEATURES), (6 * FEATURES) ** -0.5, 0.3125, (), jnp.float32)
    dilated_bias = centred(arg_keys[4], (LAYERS, FEATURES), 0.5, 3.0, (), jnp.float32)
    decode_weight = centred(arg_keys[5], (9, FEATURES), (2 * FEATURES) ** -0.5, 0.5, (), jnp.float32)
    return dict(signal=signal, encode_weight=encode_weight, encode_bias=encode_bias, dilated_weight=dilated_weight, dilated_bias=dilated_bias, decode_weight=decode_weight)


def encode_layer(padded, encode_weight, encode_bias, half_c, half_t):
    taps = []
    for row_tap in range(3):
        for lag in range(3):
            taps.append(lax.slice(padded, (row_tap, 2 - lag), (row_tap + 2 * half_c - 1, 2 - lag + 2 * half_t - 1), (2, 2)))
    stacked = jnp.stack(taps)
    before = jnp.einsum('fk,kct->fct', encode_weight, stacked, precision=lax.Precision.HIGHEST)
    return jax.nn.silu(before + encode_bias[:, None, None])


def dilated_layer(hidden, weights, bias, dilation):
    padded = jnp.pad(hidden, ((0, 0), (1, 1), (dilation, 0)))
    channels = hidden.shape[1]
    steps = hidden.shape[2]
    total = jnp.zeros(hidden.shape, jnp.float32) + bias[:, None, None]
    for row_tap in range(3):
        for lag in range(2):
            start = dilation - lag * dilation
            piece = padded[:, row_tap:row_tap + channels, start:start + steps]
            total = total + jnp.einsum('oi,ict->oct', weights[2 * row_tap + lag], piece, precision=lax.Precision.HIGHEST)
    return hidden + jax.nn.silu(total)


def assemble(maps, half_c, half_t):
    def take_part(row_tap, lag, chan_shift, time_shift):
        return maps[3 * row_tap + lag, chan_shift:chan_shift + half_c, 1 - time_shift:1 - time_shift + half_t]
    even_even = take_part(1, 0, 0, 0) + take_part(1, 2, 0, 1)
    even_odd = take_part(1, 1, 0, 0)
    odd_even = take_part(0, 0, 1, 0) + take_part(0, 2, 1, 1) + take_part(2, 0, 0, 0) + take_part(2, 2, 0, 1)
    odd_odd = take_part(0, 1, 1, 0) + take_part(2, 1, 0, 0)
    rows_even = jnp.stack([even_even, even_odd], -1)
    rows_odd = jnp.stack([odd_even, odd_odd], -1)
    return jnp.stack([rows_even, rows_odd], 1).reshape(2 * half_c, 2 * half_t)


def reference(signal, encode_weight, encode_bias, dilated_weight, dilated_bias, decode_weight):
    half_c = CH // 2
    half_t = TM // 2
    padded = jnp.pad(signal, ((1, 1), (2, 0)))
    hidden = encode_layer(padded, encode_weight, encode_bias, half_c, half_t)
    for layer in range(LAYERS):
        hidden = dilated_layer(hidden, dilated_weight[layer], dilated_bias[layer], 2 ** layer)
    maps = jnp.einsum('kf,fct->kct', decode_weight, hidden, precision=lax.Precision.HIGHEST)
    padded_maps = jnp.pad(maps, ((0, 0), (0, 1), (1, 0)))
    recon = assemble(padded_maps, half_c, half_t)
    squared = (recon - signal) ** 2
    tile_error = squared.reshape(CH // TILE_C, TILE_C, TM // TILE_T, TILE_T).mean(axis=(1, 3))
    return recon, tile_error
```

```python
import jax
import jax.numpy as jnp
from jax import lax
from jax.experimental import pallas as pl
from jax.experimental.pallas import tpu as pltpu
from jax.sharding import PartitionSpec as P

LAYERS = 6
F = 64
TILE_C = 16
TILE_T = 128
CB = 16
HB = 256
HH = 64
ROWS = HH + HB
PAIRS = (CB + 2 * LAYERS + 2) // 2
KEPT = (0, 0, 0, 0, 0, 16, 48)
HIST = 256
EDGE = 16
BF = jnp.bfloat16
F32 = jnp.float32


def split(x):
    hi = x.astype(BF)
    return hi, (x - hi.astype(F32)).astype(BF)


def from_behind(block, axis, distance):
    devices = range(lax.axis_size(axis))
    route = [(i - distance, i) for i in devices if i - distance in devices]
    return lax.ppermute(block, axis, route)


def prepare(ew_ref, dw_ref, de_ref, enc_ref, dil_ref, dec_ref, wide):
    ew = ew_ref[...]
    k = lax.broadcasted_iota(jnp.int32, (9, 256), 0)
    lane = lax.broadcasted_iota(jnp.int32, (9, 256), 1)
    base = []
    for j in range(4):
        pick = (lane // F == k % 3) & (lane % F == 3 + 2 * j + k // 3)
        base.append(
            jnp.dot(ew, pick.astype(F32), precision=lax.Precision.HIGHEST,
                    preferred_element_type=F32)
        )
    base = jnp.concatenate(base, 0).T
    none = jnp.zeros((F, 256), F32)
    for g in range(8):
        parts = []
        for b in range(3):
            piece = base[b * F : b * F + 16]
            if g < 7:
                rows = [none[: 8 * g], piece, none[: F - 16 - 8 * g]]
            else:
                rows = [none[: F - 8], piece[:8]]
            parts += [r for r in rows if r.shape[0]]
        parts.append(none)
        hi, lo = split(jnp.concatenate(parts, 0))
        enc_ref[g, 0:256] = hi
        enc_ref[g, 256:512] = hi
        enc_ref[g, 512:768] = lo
    zero = jnp.zeros((F, F), F32)
    for layer in range(LAYERS):
        odd = layer % 2
        ins = (1, 0, 3, 2) if odd else (0, 1, 2, 3)
        outs = (1, 2) if odd else (2, 1)
        for lag in range(2):
            for n, co in enumerate(outs):
                cols = [
                    dw_ref[layer, 2 * (ci - co + 1) + lag] * 0.5 if 0 <= ci - co + 1 <= 2 else zero
                    for ci in ins
                ]
                wide[pl.ds((2 * lag + n) * F, F), :] = jnp.concatenate(cols, 1)
        hi, lo = split(wide[...].T)
        dil_ref[layer, 0:256] = hi
        dil_ref[layer, 256:512] = hi
        dil_ref[layer, 512:768] = lo
    for q in range(9):
        wide[...] = jnp.zeros((256, 256), F32)
        for s in range(2):
            c = 2 * q + s
            for a in range(3):
                p = 2 * c + a - 1
                if 0 <= p < 2 * CB:
                    for b, at in enumerate((0, 32, 128)):
                        wide[at + p : at + p + 1, s * F : s * F + F] = de_ref[3 * a + b : 3 * a + b + 1, :]
        hi, lo = split(wide[:, 0:128].T)
        dec_ref[0, q * 128 : q * 128 + 128] = hi
        dec_ref[1, q * 128 : q * 128 + 128] = lo


def score(sig_ref, hist_ref, low_ref, high_ref, eb_ref, db_ref, enc_ref, dil_ref, dec_ref,
          recon_ref, err_ref, st, hid, top, low, mask, wide):
    first = lax.axis_index("fiber") == 0
    last = lax.axis_index("fiber") == lax.axis_size("fiber") - 1
    m_low = jnp.where(first, 0.0, 1.0).astype(F32)
    m_high = jnp.where(last, 0.0, 1.0).astype(F32)
    m_time = jnp.where(lax.axis_index("tm") == 0, 0.0, 1.0).astype(F32)
    pair = lax.broadcasted_iota(jnp.int32, (16, 128), 0)
    lane = lax.broadcasted_iota(jnp.int32, (16, 128), 1)
    for layer in range(LAYERS + 1):
        second = lane // F if layer % 2 == 0 else 1 - lane // F
        c = layer - LAYERS + 2 * pair + second
        mask[layer] = jnp.where(c < 0, m_low, jnp.where(c >= CB, m_high, 1.0))
    own = jnp.concatenate([hist_ref[...], sig_ref[...]], 1)
    s = jnp.concatenate([low_ref[...], own, high_ref[...]], 0)
    both = jnp.concatenate([s, pltpu.roll(s, 1, 1)], 0)
    for n in range((HIST + 2 * HB) // 128):
        st[pl.ds(n * 128, 128), :] = both[:, n * 128 : n * 128 + 128].T
    x = jnp.concatenate(
        [st[pl.ds(HIST - 2 * HH - back, ROWS, 2), :] for back in (0, 2)], 1
    )
    hi, lo = split(x)
    x = jnp.concatenate([hi, lo, hi], 1)
    eb = eb_ref[...]

    def keep(buf, i, value, layer, start):
        value = value * mask[layer, pl.ds(i, 1), :]
        value = jnp.concatenate([value[: HH - start] * m_time, value[HH - start :]], 0)
        hid[buf, i, start:ROWS] = value
        hi, lo = split(value)
        top[buf, i, start:ROWS] = hi
        low[buf, i, start:ROWS] = lo

    def encode(g, carry):
        y = jnp.dot(x, enc_ref[g], preferred_element_type=F32)
        for n in range(2):
            u = (y[:, n * 128 : n * 128 + 128] + eb) * 0.5
            keep(0, 2 * g + n, u + u * jnp.tanh(u), 0, 0)
        return carry

    lax.fori_loop(0, 8, encode, 0)
    low_half = lax.broadcasted_iota(jnp.int32, (1, 128), 1) < F
    for layer in range(LAYERS):
        d = 2**layer
        src, dst = layer % 2, 1 - layer % 2
        start = KEPT[layer + 1]
        begin = max(0, (start - d) // 16 * 16)
        bias = db_ref[layer : layer + 1, :]

        def dilated(i, carry, layer=layer, d=d, src=src, dst=dst, start=start, begin=begin, bias=bias):
            hi = [top[src, i + n, begin:ROWS] for n in range(2)]
            lo = [low[src, i + n, begin:ROWS] for n in range(2)]
            y = jnp.dot(jnp.concatenate(hi + lo + hi, 1), dil_ref[layer], preferred_element_type=F32)
            past = pltpu.roll(y[:, 128:], d, 0)[start - begin :]
            u = y[start - begin :, :128] + past + bias
            near, far = (i, i + 1) if src else (i + 1, i)
            h = jnp.where(low_half, hid[src, near, start:ROWS], hid[src, far, start:ROWS])
            keep(dst, i, h + u + u * jnp.tanh(u), layer + 1, start)
            return carry

        lax.fori_loop(0, PAIRS - 1 - layer, dilated, 0)
    start = KEPT[LAYERS]
    hi = jnp.concatenate([top[0, q, start:ROWS] for q in range(9)], 1)
    lo = jnp.concatenate([low[0, q, start:ROWS] for q in range(9)], 1)
    r = jnp.dot(hi, dec_ref[0], preferred_element_type=F32)
    r = r + jnp.dot(lo, dec_ref[0], preferred_element_type=F32)
    r = r + jnp.dot(hi, dec_ref[1], preferred_element_type=F32)
    past = pltpu.roll(r[:, 128:], 1, 0)[HH - start :]
    now = r[HH - start :, :128]
    wide[pl.ds(0, HB, 2), :] = now + past
    wide[pl.ds(1, HB, 2), :] = pltpu.roll(now, 96, 1)
    sums = []
    for n in range(2 * HB // TILE_T):
        cols = slice(n * TILE_T, n * TILE_T + TILE_T)
        out = wide[cols, :].T[: 2 * CB]
        recon_ref[:, cols] = out
        sq = (out - sig_ref[:, cols]) ** 2
        per = [jnp.sum(sq[m * TILE_C : m * TILE_C + TILE_C], keepdims=True) for m in range(2 * CB // TILE_C)]
        sums.append(jnp.concatenate(per, 0))
    err_ref[...] = jnp.concatenate(sums, 1) * (1.0 / (TILE_C * TILE_T))


def on_device(signal, encode_weight, encode_bias, dilated_weight, dilated_bias, decode_weight):
    vmem = pl.BlockSpec(memory_space=pltpu.VMEM)
    enc, dil, dec = pl.pallas_call(
        prepare,
        out_shape=(
            jax.ShapeDtypeStruct((8, 768, 256), BF),
            jax.ShapeDtypeStruct((LAYERS, 768, 256), BF),
            jax.ShapeDtypeStruct((2, 1152, 256), BF),
        ),
        in_specs=[vmem] * 3,
        out_specs=(vmem,) * 3,
        scratch_shapes=[pltpu.VMEM((256, 256), F32)],
        cost_estimate=pl.CostEstimate(flops=10**9, bytes_accessed=8 * 10**6, transcendentals=0),
        compiler_params=pltpu.CompilerParams(vmem_limit_bytes=32 * 2**20),
        name="prepare",
    )(encode_weight, dilated_weight, decode_weight)
    history = from_behind(signal[:, 2 * HB - HIST :], "tm", 1)
    whole = jnp.concatenate([history, signal], 1)
    below = from_behind(whole[2 * CB - EDGE :], "fiber", 1)
    above = from_behind(whole[:EDGE], "fiber", -1)
    eb = jnp.tile(encode_bias.reshape(1, F), (1, 2))
    db = jnp.tile(dilated_bias, (1, 2)) * 0.5
    return pl.pallas_call(
        score,
        out_shape=(
            jax.ShapeDtypeStruct((2 * CB, 2 * HB), F32),
            jax.ShapeDtypeStruct((2 * CB // TILE_C, 2 * HB // TILE_T), F32),
        ),
        in_specs=[vmem] * 9,
        out_specs=(vmem,) * 2,
        scratch_shapes=[
            pltpu.VMEM((HIST + 2 * HB, 128), F32),
            pltpu.VMEM((2, 16, ROWS, 128), F32),
            pltpu.VMEM((2, 16, ROWS, 128), BF),
            pltpu.VMEM((2, 16, ROWS, 128), BF),
            pltpu.VMEM((LAYERS + 1, 16, 128), F32),
            pltpu.VMEM((2 * HB, 128), F32),
        ],
        cost_estimate=pl.CostEstimate(flops=10**10, bytes_accessed=8 * 10**6, transcendentals=0),
        compiler_params=pltpu.CompilerParams(vmem_limit_bytes=48 * 2**20),
        name="score",
    )(signal, history, below, above, eb, db, enc, dil, dec)


def solution(mesh):
    return jax.shard_map(
        on_device,
        mesh=mesh,
        in_specs=(P("fiber", "tm"), P(), P(), P(), P(), P()),
        out_specs=(P("fiber", "tm"), P("fiber", "tm")),
        check_vma=False,
    )
```

```python
import jax
import jax.numpy as jnp
from jax import lax
from jax.experimental import pallas as pl
from jax.experimental.pallas import tpu as pltpu
from jax.sharding import PartitionSpec as P

LAYERS = 6
F = 64
TILE_C = 16
TILE_T = 128
CB = 16
HB = 256
HH = 64
ROWS = HH + HB
PAIRS = (CB + 2 * LAYERS + 2) // 2
KEPT = (0, 0, 0, 0, 0, 16, 48)
GROUP = 3
HIST = 256
EDGE = 16
BF = jnp.bfloat16
F32 = jnp.float32


def split(x):
    hi = x.astype(BF)
    return hi, (x - hi.astype(F32)).astype(BF)


def from_behind(block, axis, distance):
    devices = range(lax.axis_size(axis))
    route = [(i - distance, i) for i in devices if i - distance in devices]
    return lax.ppermute(block, axis, route)


def prepare(ew_ref, dw_ref, de_ref, enc_ref, dil_ref, dec_ref, wide):
    ew = ew_ref[...]
    k = lax.broadcasted_iota(jnp.int32, (9, 256), 0)
    lane = lax.broadcasted_iota(jnp.int32, (9, 256), 1)
    base = []
    for j in range(4):
        pick = (lane // F == k % 3) & (lane % F == 3 + 2 * j + k // 3)
        base.append(
            jnp.dot(ew, pick.astype(F32), precision=lax.Precision.HIGHEST,
                    preferred_element_type=F32)
        )
    base = jnp.concatenate(base, 0).T
    none = jnp.zeros((F, 256), F32)
    for g in range(8):
        parts = []
        for b in range(3):
            piece = base[b * F : b * F + 16]
            if g < 7:
                rows = [none[: 8 * g], piece, none[: F - 16 - 8 * g]]
            else:
                rows = [none[: F - 8], piece[:8]]
            parts += [r for r in rows if r.shape[0]]
        parts.append(none)
        hi, lo = split(jnp.concatenate(parts, 0))
        enc_ref[g, 0] = hi
        enc_ref[g, 1] = lo
    zero = jnp.zeros((F, F), F32)
    for layer in range(LAYERS):
        odd = layer % 2
        ins = (1, 0, 3, 2) if odd else (0, 1, 2, 3)
        outs = (1, 2) if odd else (2, 1)
        for lag in range(2):
            for n, co in enumerate(outs):
                cols = [
                    dw_ref[layer, 2 * (ci - co + 1) + lag] * 0.5 if 0 <= ci - co + 1 <= 2 else zero
                    for ci in ins
                ]
                wide[pl.ds((2 * lag + n) * F, F), :] = jnp.concatenate(cols, 1)
        hi, lo = split(wide[...].T)
        dil_ref[layer, 0] = hi
        dil_ref[layer, 1] = lo
    dec_ref[4, :, 128:] = jnp.zeros((2, 128, 256), BF)
    for q in range(9):
        wide[...] = jnp.zeros((256, 256), F32)
        for s in range(2):
            c = 2 * q + s
            for a in range(3):
                p = 2 * c + a - 1
                if 0 <= p < 2 * CB:
                    for b, at in enumerate((0, 32, 128)):
                        wide[at + p : at + p + 1, s * F : s * F + F] = de_ref[3 * a + b : 3 * a + b + 1, :]
        hi, lo = split(wide[:, 0:128].T)
        at = q % 2 * 128
        dec_ref[q // 2, 0, at : at + 128] = hi
        dec_ref[q // 2, 1, at : at + 128] = lo


def score(sig_ref, hist_ref, low_ref, high_ref, eb_ref, db_ref, enc_ref, dil_ref, dec_ref,
          recon_ref, err_ref, st, parts, hid, top, low, mask, wide, wide2):
    first = lax.axis_index("fiber") == 0
    last = lax.axis_index("fiber") == lax.axis_size("fiber") - 1
    m_low = jnp.where(first, 0.0, 1.0).astype(F32)
    m_high = jnp.where(last, 0.0, 1.0).astype(F32)
    m_time = jnp.where(lax.axis_index("tm") == 0, 0.0, 1.0).astype(F32)
    pair = lax.broadcasted_iota(jnp.int32, (16, 128), 0)
    lane = lax.broadcasted_iota(jnp.int32, (16, 128), 1)
    for layer in range(LAYERS + 1):
        second = lane // F if layer % 2 == 0 else 1 - lane // F
        c = layer - LAYERS + 2 * pair + second
        mask[layer] = jnp.where(c < 0, m_low, jnp.where(c >= CB, m_high, 1.0))
    own = jnp.concatenate([hist_ref[...], sig_ref[...]], 1)
    s = jnp.concatenate([low_ref[...], own, high_ref[...]], 0)
    both = jnp.concatenate([s, pltpu.roll(s, 1, 1)], 0)
    for n in range((HIST + 2 * HB) // 128):
        st[pl.ds(n * 128, 128), :] = both[:, n * 128 : n * 128 + 128].T
    x = jnp.concatenate(
        [st[pl.ds(HIST - 2 * HH - back, ROWS, 2), :] for back in (0, 2)], 1
    )
    parts[0], parts[1] = split(x)
    eb = eb_ref[...]
    low_half = lax.broadcasted_iota(jnp.int32, (1, 128), 1) < F

    def keep(buf, i, value, layer, start):
        value = value * mask[layer, i : i + 1, :]
        value = jnp.concatenate([value[: HH - start] * m_time, value[HH - start :]], 0)
        hid[buf, i, start:ROWS] = value
        hi, lo = split(value)
        top[buf, i, start:ROWS] = hi
        low[buf, i, start:ROWS] = lo

    def multiply(acc, lhs, weights):
        for n in range(2):
            pltpu.matmul_push_rhs(weights[0], 0, n)
            pltpu.matmul_push_rhs(weights[1], 1, n)
        for part, kind, load in ((0, 0, 0), (1, 0, None), (0, 1, 1)):
            for g, pieces in enumerate(lhs):
                for n in range(2):
                    pltpu.matmul_acc_lhs(acc[n][g], pieces[part][n](), load if g == 0 else None)

    def take(acc, g, rows):
        return jnp.concatenate([pltpu.matmul_pop(acc[n][g])[: rows[n]] for n in range(2)], 0)

    half = ROWS // 2

    def encode(g):
        def mm(acc):
            lhs = [[[lambda k=k, n=n: parts[k, n * half : n * half + half] for n in range(2)] for k in range(2)]]
            multiply(acc, lhs, (enc_ref[g, 0], enc_ref[g, 1]))

        def finish(acc):
            y = take(acc, 0, (half, half))
            for n in range(2):
                if 2 * g + n < PAIRS:
                    u = (y[:, n * 128 : n * 128 + 128] + eb) * 0.5
                    keep(0, 2 * g + n, u + u * jnp.tanh(u), 0, 0)

        return mm, finish

    def dilated(layer, pairs):
        d = 2**layer
        src, dst = layer % 2, 1 - layer % 2
        start = KEPT[layer + 1]
        begin = max(0, (start - d) // 16 * 16)

        def piece(ref, i, n):
            lo, hi = ((begin, half), (half, ROWS))[n]
            if begin and n == 0:
                lo = 0
            return jnp.concatenate([ref[src, i, lo:hi], ref[src, i + 1, lo:hi]], 1)

        def mm(acc):
            lhs = [[[lambda ref=ref, i=i, n=n: piece(ref, i, n) for n in range(2)] for ref in (top, low)] for i in pairs]
            multiply(acc, lhs, (dil_ref[layer, 0], dil_ref[layer, 1]))

        def finish(acc):
            bias = db_ref[layer : layer + 1, :]
            for g, i in enumerate(pairs):
                y = take(acc, g, (half, half))
                past = pltpu.roll(y[:, 128:], d, 0)[start:]
                u = y[start:, :128] + past + bias
                near, far = (i, i + 1) if src else (i + 1, i)
                h = jnp.where(low_half, hid[src, near, start:ROWS], hid[src, far, start:ROWS])
                keep(dst, i, h + u + u * jnp.tanh(u), layer + 1, start)

        return mm, finish

    def decode():
        edges = ((KEPT[LAYERS], 192), (192, ROWS))

        def mm(acc):
            def piece(ref, q, n):
                lo, hi = edges[n]
                two = [ref[0, i, lo:hi] for i in (q, min(q + 1, 8))]
                return jnp.concatenate(two, 1)
            for q in range(5):
                for n in range(2):
                    pltpu.matmul_push_rhs(dec_ref[q, 0], 0, n)
                    pltpu.matmul_push_rhs(dec_ref[q, 1], 1, n)
                for ref, load in ((top, 0), (low, None), (top, 1)):
                    for n in range(2):
                        pltpu.matmul_acc_lhs(acc[n], piece(ref, 2 * q, n), load)

        return mm

    tasks = [encode(g) for g in range(8)]
    for layer in range(LAYERS):
        count = PAIRS - 1 - layer
        for i in range(0, count, GROUP):
            tasks.append(dilated(layer, range(i, min(i + GROUP, count))))

    def run(*refs):
        sets = [[refs[(2 * s + n) * GROUP : (2 * s + n + 1) * GROUP] for n in range(2)] for s in range(2)]
        tasks[0][0](sets[0])
        for k, (_, finish) in enumerate(tasks):
            if k + 1 < len(tasks):
                tasks[k + 1][0](sets[(k + 1) % 2])
            finish(sets[k % 2])

    accs = [pltpu.ACC(n)((half, 256), F32) for s in range(2) for n in range(2) for g in range(GROUP)]
    pl.run_scoped(run, *accs)
    start = KEPT[LAYERS]

    def last(a0, a1):
        decode()((a0, a1))
        sums = jnp.concatenate([pltpu.matmul_pop(a0), pltpu.matmul_pop(a1)], 0)
        wide2[...] = sums

    pl.run_scoped(last, pltpu.ACC(0)((192 - start, 256), F32), pltpu.ACC(1)((ROWS - 192, 256), F32))
    r = wide2[...]
    past = pltpu.roll(r[:, 128:], 1, 0)[HH - start :]
    now = r[HH - start :, :128]
    wide[pl.ds(0, HB, 2), :] = now + past
    wide[pl.ds(1, HB, 2), :] = pltpu.roll(now, 96, 1)
    sums = []
    for n in range(2 * HB // TILE_T):
        cols = slice(n * TILE_T, n * TILE_T + TILE_T)
        out = wide[cols, :].T[: 2 * CB]
        recon_ref[:, cols] = out
        sq = (out - sig_ref[:, cols]) ** 2
        per = [jnp.sum(sq[m * TILE_C : m * TILE_C + TILE_C], keepdims=True) for m in range(2 * CB // TILE_C)]
        sums.append(jnp.concatenate(per, 0))
    err_ref[...] = jnp.concatenate(sums, 1) * (1.0 / (TILE_C * TILE_T))


def on_device(signal, encode_weight, encode_bias, dilated_weight, dilated_bias, decode_weight):
    vmem = pl.BlockSpec(memory_space=pltpu.VMEM)
    enc, dil, dec = pl.pallas_call(
        prepare,
        out_shape=(
            jax.ShapeDtypeStruct((8, 2, 256, 256), BF),
            jax.ShapeDtypeStruct((LAYERS, 2, 256, 256), BF),
            jax.ShapeDtypeStruct((5, 2, 256, 256), BF),
        ),
        in_specs=[vmem] * 3,
        out_specs=(vmem,) * 3,
        scratch_shapes=[pltpu.VMEM((256, 256), F32)],
        cost_estimate=pl.CostEstimate(flops=10**9, bytes_accessed=8 * 10**6, transcendentals=0),
        compiler_params=pltpu.CompilerParams(vmem_limit_bytes=32 * 2**20),
        name="prepare",
    )(encode_weight, dilated_weight, decode_weight)
    history = from_behind(signal[:, 2 * HB - HIST :], "tm", 1)
    whole = jnp.concatenate([history, signal], 1)
    below = from_behind(whole[2 * CB - EDGE :], "fiber", 1)
    above = from_behind(whole[:EDGE], "fiber", -1)
    eb = jnp.tile(encode_bias.reshape(1, F), (1, 2))
    db = jnp.tile(dilated_bias, (1, 2)) * 0.5
    return pl.pallas_call(
        score,
        out_shape=(
            jax.ShapeDtypeStruct((2 * CB, 2 * HB), F32),
            jax.ShapeDtypeStruct((2 * CB // TILE_C, 2 * HB // TILE_T), F32),
        ),
        in_specs=[vmem] * 9,
        out_specs=(vmem,) * 2,
        scratch_shapes=[
            pltpu.VMEM((HIST + 2 * HB, 128), F32),
            pltpu.VMEM((2, ROWS, 256), BF),
            pltpu.VMEM((2, 16, ROWS, 128), F32),
            pltpu.VMEM((2, 16, ROWS, 128), BF),
            pltpu.VMEM((2, 16, ROWS, 128), BF),
            pltpu.VMEM((LAYERS + 1, 16, 128), F32),
            pltpu.VMEM((2 * HB, 128), F32),
            pltpu.VMEM((ROWS - KEPT[LAYERS], 256), F32),
        ],
        cost_estimate=pl.CostEstimate(flops=10**10, bytes_accessed=8 * 10**6, transcendentals=0),
        compiler_params=pltpu.CompilerParams(vmem_limit_bytes=48 * 2**20),
        name="score",
    )(signal, history, below, above, eb, db, enc, dil, dec)


def solution(mesh):
    return jax.shard_map(
        on_device,
        mesh=mesh,
        in_specs=(P("fiber", "tm"), P(), P(), P(), P(), P()),
        out_specs=(P("fiber", "tm"), P("fiber", "tm")),
        check_vma=False,
    )
```

```python
import jax
import jax.numpy as jnp
from jax import lax
from jax.experimental import pallas as pl
from jax.experimental.pallas import tpu as pltpu
from jax.sharding import PartitionSpec as P

LAYERS = 6
F = 64
TILE_C = 16
TILE_T = 128
CB = 16
HB = 256
HH = 64
ROWS = HH + HB
PAIRS = (CB + 2 * LAYERS + 2) // 2
KEPT = (0, 0, 0, 0, 0, 16, 48)
GROUP = 3
HIST = 256
EDGE = 16
BF = jnp.bfloat16
F32 = jnp.float32


def split(x):
    hi = x.astype(BF)
    return hi, (x - hi.astype(F32)).astype(BF)


def from_behind(block, axis, distance):
    devices = range(lax.axis_size(axis))
    route = [(i - distance, i) for i in devices if i - distance in devices]
    return lax.ppermute(block, axis, route)


def exchange(block, axis, first):
    lows = range(first, lax.axis_size(axis) - 1, 2)
    return lax.ppermute(block, axis, [p for i in lows for p in ((i, i + 1), (i + 1, i))])


def encoder_weights(small_ref, enc_ref, wide):
    ew = small_ref[0:9] * 0.5
    wide[...] = jnp.zeros(wide.shape, F32)
    for j in range(4):
        for a in range(3):
            for b in range(3):
                wide[b, 3 + 2 * j + a : 4 + 2 * j + a, j * F : j * F + F] = ew[3 * a + b : 3 * a + b + 1, :]
    none = jnp.zeros((F, 256), F32)
    for g in range(8):
        parts = []
        for b in range(3):
            piece = wide[b]
            if g < 7:
                rows = [none[: 8 * g], piece, none[: F - 16 - 8 * g]]
            else:
                rows = [none[: F - 8], piece[:8]]
            parts += [r for r in rows if r.shape[0]]
        parts.append(none)
        enc_ref[g, 0], enc_ref[g, 1] = split(jnp.concatenate(parts, 0))


def layer_weights(layer, dw_ref, dil_ref):
    zero = jnp.zeros((F, F), F32)
    ins = (1, 0, 3, 2) if layer % 2 else (0, 1, 2, 3)
    outs = (1, 2) if layer % 2 else (2, 1)
    rows = []
    for lag in range(2):
        for co in outs:
            cols = [
                dw_ref[layer, 2 * (ci - co + 1) + lag] * 0.5 if 0 <= ci - co + 1 <= 2 else zero
                for ci in ins
            ]
            rows.append(jnp.concatenate(cols, 1))
    dil_ref[layer, 0], dil_ref[layer, 1] = split(jnp.concatenate(rows, 0).T)


def decoder_weights(de, dec_ref, wide):
    wide[...] = jnp.zeros(wide.shape, F32)
    for c in range(CB + 1):
        for a in range(3):
            p = 2 * c + a - 1
            if 0 <= p < 2 * CB:
                for b, at in enumerate((0, 32, 128)):
                    k = c % 4 * F
                    wide[c // 4, at + p : at + p + 1, k : k + F] = de[3 * a + b : 3 * a + b + 1, :]
    for q in range(5):
        dec_ref[q, 0], dec_ref[q, 1] = split(wide[q].T)


def score(sig_ref, hist_ref, near_ref, far_ref, small_ref, dw_ref, enc_ref,
          recon_ref, err_ref, st, parts, hid, top, low, mask, wide, wide2, wide3, dil_ref, dec_ref):
    small = small_ref[...]
    bias = jnp.concatenate([small[18:25], small[18:25]], 1) * 0.5
    layer_weights(0, dw_ref, dil_ref)
    first = lax.axis_index("fiber") == 0
    last = lax.axis_index("fiber") == lax.axis_size("fiber") - 1
    m_low = jnp.where(first, 0.0, 1.0).astype(F32)
    m_high = jnp.where(last, 0.0, 1.0).astype(F32)
    m_time = jnp.where(lax.axis_index("tm") == 0, 0.0, 1.0).astype(F32)
    pair = lax.broadcasted_iota(jnp.int32, (16, 128), 0)
    lane = lax.broadcasted_iota(jnp.int32, (16, 128), 1)
    for layer in range(LAYERS + 1):
        second = lane // F if layer % 2 == 0 else 1 - lane // F
        c = layer - LAYERS + 2 * pair + second
        mask[layer] = jnp.where(c < 0, m_low, jnp.where(c >= CB, m_high, 1.0))
    own = jnp.concatenate([hist_ref[:, 2 * HB - HIST :], sig_ref[...]], 1)
    even = lax.axis_index("fiber") % 2 == 0
    near, far = near_ref[...], far_ref[...]
    s = jnp.concatenate([jnp.where(even, far, near), own, jnp.where(even, near, far)], 0)
    both = jnp.concatenate([s, pltpu.roll(s, 1, 1)], 0)
    for n in range((HIST + 2 * HB) // 128):
        st[pl.ds(n * 128, 128), :] = both[:, n * 128 : n * 128 + 128].T
    x = jnp.concatenate(
        [st[pl.ds(HIST - 2 * HH - back, ROWS, 2), :] for back in (0, 2)], 1
    )
    parts[0], parts[1] = split(x)
    eb = bias[0:1]
    low_half = lax.broadcasted_iota(jnp.int32, (1, 128), 1) < F

    def keep(buf, i, value, layer, start):
        value = value * mask[layer, i : i + 1, :]
        value = jnp.concatenate([value[: HH - start] * m_time, value[HH - start :]], 0)
        hid[buf, i, start:ROWS] = value
        hi, lo = split(value)
        top[buf, i, start:ROWS] = hi
        low[buf, i, start:ROWS] = lo

    def multiply(acc, lhs, weights):
        for n in range(2):
            pltpu.matmul_push_rhs(weights[0], 0, n)
            pltpu.matmul_push_rhs(weights[1], 1, n)
        for part, kind, load in ((0, 0, 0), (1, 0, None), (0, 1, 1)):
            for g, pieces in enumerate(lhs):
                for n in range(2):
                    pltpu.matmul_acc_lhs(acc[n][g], pieces[part][n](), load if g == 0 else None)

    def take(acc, g, rows):
        return jnp.concatenate([pltpu.matmul_pop(acc[n][g])[: rows[n]] for n in range(2)], 0)

    half = ROWS // 2

    def encode(g):
        def mm(acc):
            lhs = [[[lambda k=k, n=n: parts[k, n * half : n * half + half] for n in range(2)] for k in range(2)]]
            multiply(acc, lhs, (enc_ref[g, 0], enc_ref[g, 1]))

        def finish(acc):
            y = take(acc, 0, (half, half))
            for n in range(2):
                if 2 * g + n < PAIRS:
                    u = y[:, n * 128 : n * 128 + 128] + eb
                    keep(0, 2 * g + n, u + u * jnp.tanh(u), 0, 0)

        return mm, finish

    def dilated(layer, pairs):
        d = 2**layer
        src, dst = layer % 2, 1 - layer % 2
        start = KEPT[layer + 1]
        begin = max(0, (start - d) // 16 * 16)

        def piece(ref, i, n):
            lo, hi = ((begin, half), (half, ROWS))[n]
            if begin and n == 0:
                lo = 0
            return jnp.concatenate([ref[src, i, lo:hi], ref[src, i + 1, lo:hi]], 1)

        def mm(acc):
            lhs = [[[lambda ref=ref, i=i, n=n: piece(ref, i, n) for n in range(2)] for ref in (top, low)] for i in pairs]
            multiply(acc, lhs, (dil_ref[layer, 0], dil_ref[layer, 1]))

        def finish(acc):
            b = bias[layer + 1 : layer + 2]
            for g, i in enumerate(pairs):
                y = take(acc, g, (half, half))
                past = pltpu.roll(y[:, 128:], d, 0)[start:]
                u = y[start:, :128] + past + b
                near, far = (i, i + 1) if src else (i + 1, i)
                h = jnp.where(low_half, hid[src, near, start:ROWS], hid[src, far, start:ROWS])
                keep(dst, i, h + u + u * jnp.tanh(u), layer + 1, start)

        return mm, finish

    def decode():
        edges = ((KEPT[LAYERS], 192), (192, ROWS))

        def mm(acc):
            def piece(ref, q, n):
                lo, hi = edges[n]
                two = [ref[0, i, lo:hi] for i in (q, min(q + 1, 8))]
                return jnp.concatenate(two, 1)
            for q in range(5):
                for n in range(2):
                    pltpu.matmul_push_rhs(dec_ref[q, 0], 0, n)
                    pltpu.matmul_push_rhs(dec_ref[q, 1], 1, n)
                for ref, load in ((top, 0), (low, None), (top, 1)):
                    for n in range(2):
                        pltpu.matmul_acc_lhs(acc[n], piece(ref, 2 * q, n), load)

        return mm

    ahead = {}
    tasks = [encode(g) for g in range(8)]
    for layer in range(LAYERS):
        count = PAIRS - 1 - layer
        for i in range(0, count, GROUP):
            tasks.append(dilated(layer, range(i, min(i + GROUP, count))))
            if i == 0:
                if layer + 1 < LAYERS:
                    ahead[len(tasks)] = lambda layer=layer: layer_weights(layer + 1, dw_ref, dil_ref)
                else:
                    ahead[len(tasks)] = lambda: decoder_weights(small[9:18], dec_ref, wide3)

    def run(*refs):
        sets = [[refs[(2 * s + n) * GROUP : (2 * s + n + 1) * GROUP] for n in range(2)] for s in range(2)]
        tasks[0][0](sets[0])
        for k, (_, finish) in enumerate(tasks):
            if k in ahead:
                ahead[k]()
            if k + 1 < len(tasks):
                tasks[k + 1][0](sets[(k + 1) % 2])
            finish(sets[k % 2])

    accs = [pltpu.ACC(n)((half, 256), F32) for s in range(2) for n in range(2) for g in range(GROUP)]
    pl.run_scoped(run, *accs)
    start = KEPT[LAYERS]

    def last(a0, a1):
        decode()((a0, a1))
        sums = jnp.concatenate([pltpu.matmul_pop(a0), pltpu.matmul_pop(a1)], 0)
        wide2[...] = sums

    pl.run_scoped(last, pltpu.ACC(0)((192 - start, 256), F32), pltpu.ACC(1)((ROWS - 192, 256), F32))
    r = wide2[...]
    past = pltpu.roll(r[:, 128:], 1, 0)[HH - start :]
    now = r[HH - start :, :128]
    wide[pl.ds(0, HB, 2), :] = now + past
    wide[pl.ds(1, HB, 2), :] = pltpu.roll(now, 96, 1)
    sums = []
    for n in range(2 * HB // TILE_T):
        cols = slice(n * TILE_T, n * TILE_T + TILE_T)
        out = wide[cols, :].T[: 2 * CB]
        recon_ref[:, cols] = out
        sq = (out - sig_ref[:, cols]) ** 2
        per = [jnp.sum(sq[m * TILE_C : m * TILE_C + TILE_C], keepdims=True) for m in range(2 * CB // TILE_C)]
        sums.append(jnp.concatenate(per, 0))
    err_ref[...] = jnp.concatenate(sums, 1) * (1.0 / (TILE_C * TILE_T))


def on_device(signal, encode_weight, encode_bias, dilated_weight, dilated_bias, decode_weight):
    vmem = pl.BlockSpec(memory_space=pltpu.VMEM)
    history = from_behind(signal, "tm", 1)
    small = jnp.concatenate(
        [encode_weight.T, decode_weight, encode_bias.reshape(1, F), dilated_bias], 0
    )
    enc = pl.pallas_call(
        encoder_weights,
        out_shape=jax.ShapeDtypeStruct((8, 2, 256, 256), BF),
        in_specs=[vmem],
        out_specs=vmem,
        scratch_shapes=[pltpu.VMEM((3, 16, 256), F32)],
        cost_estimate=pl.CostEstimate(flops=10**9, bytes_accessed=2 * 10**6, transcendentals=0),
        compiler_params=pltpu.CompilerParams(vmem_limit_bytes=16 * 2**20),
        name="encoder_weights",
    )(small)
    history, enc = lax.optimization_barrier((history, enc))
    even = lax.axis_index("fiber") % 2 == 0
    past = history[:, 2 * HB - HIST :]
    bottom, top = (jnp.concatenate([past[rows], signal[rows]], 1) for rows in (slice(0, EDGE), slice(2 * CB - EDGE, 2 * CB)))
    far = exchange(jnp.where(even, bottom, top), "fiber", 1)
    near = exchange(jnp.where(even, top, bottom), "fiber", 0)
    return pl.pallas_call(
        score,
        out_shape=(
            jax.ShapeDtypeStruct((2 * CB, 2 * HB), F32),
            jax.ShapeDtypeStruct((2 * CB // TILE_C, 2 * HB // TILE_T), F32),
        ),
        in_specs=[vmem] * 7,
        out_specs=(vmem,) * 2,
        scratch_shapes=[
            pltpu.VMEM((HIST + 2 * HB, 128), F32),
            pltpu.VMEM((2, ROWS, 256), BF),
            pltpu.VMEM((2, 16, ROWS, 128), F32),
            pltpu.VMEM((2, 16, ROWS, 128), BF),
            pltpu.VMEM((2, 16, ROWS, 128), BF),
            pltpu.VMEM((LAYERS + 1, 16, 128), F32),
            pltpu.VMEM((2 * HB, 128), F32),
            pltpu.VMEM((ROWS - KEPT[LAYERS], 256), F32),
            pltpu.VMEM((5, 256, 256), F32),
            pltpu.VMEM((LAYERS, 2, 256, 256), BF),
            pltpu.VMEM((5, 2, 256, 256), BF),
        ],
        cost_estimate=pl.CostEstimate(flops=10**10, bytes_accessed=8 * 10**6, transcendentals=0),
        compiler_params=pltpu.CompilerParams(vmem_limit_bytes=48 * 2**20),
        name="score",
    )(signal, history, near, far, small, dilated_weight, enc)


def solution(mesh):
    return jax.shard_map(
        on_device,
        mesh=mesh,
        in_specs=(P("fiber", "tm"), P(), P(), P(), P(), P()),
        out_specs=(P("fiber", "tm"), P("fiber", "tm")),
        check_vma=False,
    )
```

```python
import functools

import jax
import jax.numpy as jnp
from jax import lax
from jax.experimental import pallas as pl
from jax.experimental.pallas import tpu as pltpu
from jax.sharding import PartitionSpec as P

LAYERS = 6
F = 64
TILE_C = 16
TILE_T = 128
CB = 16
HB = 256
HH = 64
ROWS = HH + HB
PAIRS = (CB + 2 * LAYERS + 2) // 2
LATER = ((64, 320), (64, 320), (64, 320), (64, 320), (80, 320), (96, 320), (128, 320))
EARLIER = ((0, 80), (0, 80), (0, 80), (0, 80), (0, 80), (16, 96), (48, 128))
CHUNK = 16
SLOTS = 32
HIST = 256
EDGE = 16
BF = jnp.bfloat16
F32 = jnp.float32


def split(x):
    hi = x.astype(BF)
    return hi, (x - hi.astype(F32)).astype(BF)


def from_behind(block, axis, distance):
    devices = range(lax.axis_size(axis))
    route = [(i - distance, i) for i in devices if i - distance in devices]
    return lax.ppermute(block, axis, route)


def exchange(block, axis, first):
    lows = range(first, lax.axis_size(axis) - 1, 2)
    return lax.ppermute(block, axis, [p for i in lows for p in ((i, i + 1), (i + 1, i))])


def encoder_weights(small_ref, enc_ref, wide):
    ew = small_ref[0:9] * 0.5
    wide[...] = jnp.zeros(wide.shape, F32)
    for j in range(4):
        for a in range(3):
            for b in range(3):
                wide[b, 3 + 2 * j + a : 4 + 2 * j + a, j * F : j * F + F] = ew[3 * a + b : 3 * a + b + 1, :]
    none = jnp.zeros((F, 256), F32)
    for g in range(8):
        parts = []
        for b in range(3):
            piece = wide[b]
            if g < 7:
                rows = [none[: 8 * g], piece, none[: F - 16 - 8 * g]]
            else:
                rows = [none[: F - 8], piece[:8]]
            parts += [r for r in rows if r.shape[0]]
        parts.append(none)
        enc_ref[g, 0], enc_ref[g, 1] = split(jnp.concatenate(parts, 0))


def layer_weights(layer, dw_ref, dil_ref):
    zero = jnp.zeros((F, F), F32)
    ins = (1, 0, 3, 2) if layer % 2 else (0, 1, 2, 3)
    outs = (1, 2) if layer % 2 else (2, 1)
    rows = []
    for lag in range(2):
        for co in outs:
            cols = [
                dw_ref[layer, 2 * (ci - co + 1) + lag] * 0.5 if 0 <= ci - co + 1 <= 2 else zero
                for ci in ins
            ]
            rows.append(jnp.concatenate(cols, 1))
    dil_ref[layer, 0], dil_ref[layer, 1] = split(jnp.concatenate(rows, 0).T)


def decoder_weights(de, dec_ref, wide):
    wide[...] = jnp.zeros(wide.shape, F32)
    for c in range(CB + 1):
        for a in range(3):
            p = 2 * c + a - 1
            if 0 <= p < 2 * CB:
                for b in range(3):
                    k, at = c % 4 * F, b * 2 * CB + p
                    wide[c // 4, at : at + 1, k : k + F] = de[3 * a + b : 3 * a + b + 1, :]
    for q in range(5):
        hi, lo = split(wide[q].T)
        dec_ref[q] = jnp.concatenate([hi, lo], 1)


def edge_masks(mask):
    m_low = jnp.where(lax.axis_index("fiber") == 0, 0.0, 1.0).astype(F32)
    m_high = jnp.where(lax.axis_index("fiber") == lax.axis_size("fiber") - 1, 0.0, 1.0).astype(F32)
    pair = lax.broadcasted_iota(jnp.int32, (16, 128), 0)
    lane = lax.broadcasted_iota(jnp.int32, (16, 128), 1)
    for layer in range(LAYERS + 1):
        second = lane // F if layer % 2 == 0 else 1 - lane // F
        c = layer - LAYERS + 2 * pair + second
        mask[layer] = jnp.where(c < 0, m_low, jnp.where(c >= CB, m_high, 1.0))


def gather_taps(s, st, first, begin, count, parts, groups):
    both = jnp.concatenate([s, pltpu.roll(s, 1, 1)], 0)
    for n in range(s.shape[1] // 128):
        st[pl.ds(first + n * 128, 128), :] = both[:, n * 128 : n * 128 + 128].T
    x = [st[pl.ds(HIST + 2 * (begin - HH) - back, count, 2), :] for back in (0, 2)]
    for g in range(groups):
        rolled = [pltpu.roll(half, 128 - 8 * g, 1) if g else half for half in x]
        parts[g, 0, begin : begin + count], parts[g, 1, begin : begin + count] = split(jnp.concatenate(rolled, 1))


def network(ranges, parts, hid, top, low, mask, bias, enc_ref, dil_ref, dec_ref, encodes, group, ahead, kept, finished):
    eb = bias[0:1]
    low_half = lax.broadcasted_iota(jnp.int32, (1, 128), 1) < F
    m_time = jnp.where(lax.axis_index("tm") == 0, 0.0, 1.0).astype(F32)

    def keep(buf, i, value, layer):
        start, end = ranges[layer]
        value = value * mask[layer, i : i + 1, :]
        if start < HH:
            value = jnp.concatenate([value[: HH - start] * m_time, value[HH - start :]], 0)
        hid[buf, i, start:end] = value
        top[buf, i, start:end], low[buf, i, start:end] = split(value)
        kept(layer, i, value)

    def chunks(pairs, begin, end):
        units = [(i, r) for i in pairs for r in range(begin, end, CHUNK)]
        half = (len(units) + 1) // 2
        return units[:half], units[half:]

    def multiply(acc, units, piece, steps):
        for step, weights in enumerate(steps):
            for n in range(2):
                for k, matrix in enumerate(weights):
                    pltpu.matmul_push_rhs(matrix, k, n)
            for part, load in ((0, 0), (1, None), (0, 1))[: len(weights) + 1]:
                for n in range(2):
                    for slot, unit in enumerate(units[n]):
                        pltpu.matmul_acc_lhs(acc[n][slot], piece(part, step, unit), load if slot == 0 else None)

    def take(acc, units, i):
        out = [pltpu.matmul_pop(acc[n][slot]) for n in range(2) for slot, unit in enumerate(units[n]) if unit[0] == i]
        return jnp.concatenate(out, 0)

    def encode(groups):
        units = chunks(groups, *ranges[0])

        def mm(acc):
            g, same = (0, parts.shape[0] == 1) if len(groups) > 1 else (groups[0], True)
            multiply(acc, units, lambda part, step, unit: parts[0 if same else unit[0], part, unit[1] : unit[1] + CHUNK],
                     ((enc_ref[g, 0], enc_ref[g, 1]),))

        def finish(acc):
            for g in groups:
                y = take(acc, units, g)
                for n in range(2):
                    if 2 * g + n < PAIRS:
                        u = y[:, n * 128 : n * 128 + 128] + eb
                        keep(0, 2 * g + n, u + u * jnp.tanh(u), 0)

        return mm, finish

    def dilated(layer, pairs):
        d = 2**layer
        src, dst = layer % 2, 1 - layer % 2
        start, end = ranges[layer + 1]
        begin = max(ranges[layer][0], (start - d) // CHUNK * CHUNK)
        units = chunks(pairs, begin, end)

        def piece(part, step, unit):
            i, r = unit
            ref = low if part else top
            return jnp.concatenate([ref[src, i, r : r + CHUNK], ref[src, i + 1, r : r + CHUNK]], 1)

        def mm(acc):
            multiply(acc, units, piece, ((dil_ref[layer, 0], dil_ref[layer, 1]),))

        def finish(acc):
            for i in pairs:
                y = take(acc, units, i)
                past = pltpu.roll(y[:, 128:], d, 0)[start - begin :]
                u = y[start - begin :, :128] + past + bias[layer + 1 : layer + 2]
                near, far = (i, i + 1) if src else (i + 1, i)
                h = jnp.where(low_half, hid[src, near, start:end], hid[src, far, start:end])
                keep(dst, i, h + u + u * jnp.tanh(u), layer + 1)

        return mm, finish

    def decode():
        units = chunks((0,), *ranges[LAYERS])

        def piece(part, step, unit):
            ref, r = low if part else top, unit[1]
            return jnp.concatenate([ref[0, i, r : r + CHUNK] for i in (2 * step, min(2 * step + 1, 8))], 1)

        def mm(acc):
            multiply(acc, units, piece, [(dec_ref[q],) for q in range(5)])

        def finish(acc):
            y = take(acc, units, 0)
            finished(y[:, :128] + y[:, 128:])

        return mm, finish

    tasks = [encode(range(g, g + encodes)) for g in range(0, 8, encodes)]
    for layer in range(LAYERS):
        count = PAIRS - 1 - layer
        tasks += [dilated(layer, range(i, min(i + group, count))) for i in range(0, count, group)]
        tasks.append(lambda layer=layer: ahead(layer))
    tasks.append(decode())

    def run(*refs):
        sets = [[refs[(2 * s + n) * SLOTS : (2 * s + n + 1) * SLOTS] for n in range(2)] for s in range(2)]
        waiting, turn = None, 0
        for task in tasks:
            if callable(task):
                task()
                continue
            if task is tasks[-1] and waiting:
                waiting()
                waiting = None
            mm, finish = task
            mm(sets[turn])
            if waiting:
                waiting()
            waiting = functools.partial(finish, sets[turn])
            turn = 1 - turn
        waiting()

    pl.run_scoped(run, *[pltpu.ACC(n)((CHUNK, 256), F32) for s in range(2) for n in range(2) for k in range(SLOTS)])


def later(s_ref, small_ref, dw_ref, enc_ref, sums_ref, h4_ref, h5_ref, dil_ref, dec_ref, st, hid, top, low, mask, parts, wide):
    small = small_ref[...]
    bias = jnp.concatenate([small[18:25], small[18:25]], 1) * 0.5
    layer_weights(0, dw_ref, dil_ref)
    edge_masks(mask)
    st[HIST - 8 : HIST, :] = jnp.zeros((8, 128), F32)
    gather_taps(s_ref[...], st, HIST, HH, HB, parts, 1)

    def ahead(layer):
        if layer + 1 < LAYERS:
            layer_weights(layer + 1, dw_ref, dil_ref)
        if layer == 2:
            decoder_weights(small[9:18], dec_ref, wide)

    def kept(layer, i, value):
        if layer == 4:
            h4_ref[i] = value[:16]
        if layer == 5:
            h5_ref[i] = value[:32]

    def finished(sums):
        sums_ref[...] = sums

    network(LATER, parts, hid, top, low, mask, bias, enc_ref, dil_ref, dec_ref, 1, 3, ahead, kept, finished)


def earlier(s_ref, hist_ref, small_ref, enc_ref, sums_ref, h4_ref, h5_ref, dil_ref, dec_ref,
            recon_ref, err_ref, st, hid, top, low, mask, parts, wide, whole):
    small = small_ref[...]
    bias = jnp.concatenate([small[18:25], small[18:25]], 1) * 0.5
    edge_masks(mask)
    gather_taps(jnp.concatenate([hist_ref[...], s_ref[:, :128]], 1), st, 0, 0, EARLIER[0][1], parts, 8)
    for buf, ref, begin, end in ((0, h4_ref, 80, 96), (1, h5_ref, 96, 128)):
        for i in range(ref.shape[0]):
            value = ref[i]
            hid[buf, i, begin:end] = value
            top[buf, i, begin:end], low[buf, i, begin:end] = split(value)

    base = EARLIER[LAYERS][0]
    whole[EARLIER[LAYERS][1] - base :, :] = sums_ref[...]

    def scores(tiles):
        begin, count = HH - base + tiles[0] * TILE_T // 2, len(tiles) * TILE_T // 2
        now, past = whole[begin : begin + count, :], whole[begin - 1 : begin - 1 + count, :]
        wide[pl.ds(tiles[0] * TILE_T, count, 2), :] = now + pltpu.roll(past, 128 - 4 * CB, 1)
        wide[pl.ds(tiles[0] * TILE_T + 1, count, 2), :] = pltpu.roll(now, 128 - 2 * CB, 1)
        for n in tiles:
            cols = slice(n * TILE_T, n * TILE_T + TILE_T)
            out = wide[cols, :].T[: 2 * CB]
            recon_ref[:, cols] = out
            sq = (out - s_ref[EDGE : EDGE + 2 * CB, cols]) ** 2
            per = [jnp.sum(sq[m * TILE_C : m * TILE_C + TILE_C], keepdims=True) for m in range(2 * CB // TILE_C)]
            err_ref[:, n : n + 1] = jnp.concatenate(per, 0) * (1.0 / (TILE_C * TILE_T))

    def ahead(layer):
        if layer == 1:
            scores((2, 3))

    def finished(value):
        whole[: EARLIER[LAYERS][1] - base, :] = value

    network(EARLIER, parts, hid, top, low, mask, bias, enc_ref, dil_ref, dec_ref, 4, 4, ahead,
            lambda layer, i, value: None, finished)
    scores((0, 1))


def on_device(signal, encode_weight, encode_bias, dilated_weight, dilated_bias, decode_weight):
    vmem = pl.BlockSpec(memory_space=pltpu.VMEM)
    far = exchange(signal, "fiber", 1)
    small = jnp.concatenate(
        [encode_weight.T, decode_weight, encode_bias.reshape(1, F), dilated_bias], 0
    )
    own, small = lax.optimization_barrier((signal, small))
    near = exchange(own, "fiber", 0)
    enc = pl.pallas_call(
        encoder_weights,
        out_shape=jax.ShapeDtypeStruct((8, 2, 256, 256), BF),
        in_specs=[vmem],
        out_specs=vmem,
        scratch_shapes=[pltpu.VMEM((3, 16, 256), F32)],
        cost_estimate=pl.CostEstimate(flops=10**9, bytes_accessed=2 * 10**6, transcendentals=0),
        compiler_params=pltpu.CompilerParams(vmem_limit_bytes=16 * 2**20),
        name="encoder_weights",
    )(small)
    near, far, enc = lax.optimization_barrier((near, far, enc))
    even = lax.axis_index("fiber") % 2 == 0
    below = jnp.where(even, far[2 * CB - EDGE :], near[2 * CB - EDGE :])
    above = jnp.where(even, near[:EDGE], far[:EDGE])
    section = jnp.concatenate([below, signal, above], 0)
    history = from_behind(section[:, 2 * HB - HIST :], "tm", 1)
    scratch = [
        pltpu.VMEM((HIST + 2 * HB, 128), F32),
        pltpu.VMEM((2, 16, ROWS, 128), F32),
        pltpu.VMEM((2, 16, ROWS, 128), BF),
        pltpu.VMEM((2, 16, ROWS, 128), BF),
        pltpu.VMEM((LAYERS + 1, 16, 128), F32),
    ]
    params = pltpu.CompilerParams(vmem_limit_bytes=32 * 2**20)
    sums, h4, h5, dil, dec = pl.pallas_call(
        later,
        out_shape=(
            jax.ShapeDtypeStruct((LATER[LAYERS][1] - LATER[LAYERS][0], 128), F32),
            jax.ShapeDtypeStruct((PAIRS - 4, 16, 128), F32),
            jax.ShapeDtypeStruct((PAIRS - 5, 32, 128), F32),
            jax.ShapeDtypeStruct((LAYERS, 2, 256, 256), BF),
            jax.ShapeDtypeStruct((5, 256, 256), BF),
        ),
        in_specs=[vmem] * 4,
        out_specs=(vmem,) * 5,
        scratch_shapes=scratch + [pltpu.VMEM((1, 2, ROWS, 256), BF), pltpu.VMEM((5, 128, 256), F32)],
        cost_estimate=pl.CostEstimate(flops=8 * 10**9, bytes_accessed=8 * 10**6, transcendentals=0),
        compiler_params=params,
        name="later",
    )(section, small, dilated_weight, enc)
    return pl.pallas_call(
        earlier,
        out_shape=(
            jax.ShapeDtypeStruct((2 * CB, 2 * HB), F32),
            jax.ShapeDtypeStruct((2 * CB // TILE_C, 2 * HB // TILE_T), F32),
        ),
        in_specs=[vmem] * 9,
        out_specs=(vmem,) * 2,
        scratch_shapes=scratch
        + [pltpu.VMEM((8, 2, EARLIER[0][1], 256), BF), pltpu.VMEM((2 * HB, 128), F32), pltpu.VMEM((ROWS - EARLIER[LAYERS][0], 128), F32)],
        cost_estimate=pl.CostEstimate(flops=2 * 10**9, bytes_accessed=8 * 10**6, transcendentals=0),
        compiler_params=params,
        name="earlier",
    )(section, history, small, enc, sums, h4, h5, dil, dec)


def solution(mesh):
    return jax.shard_map(
        on_device,
        mesh=mesh,
        in_specs=(P("fiber", "tm"), P(), P(), P(), P(), P()),
        out_specs=(P("fiber", "tm"), P("fiber", "tm")),
        check_vma=False,
    )
```

```python
import functools

import jax
import jax.numpy as jnp
from jax import lax
from jax.experimental import pallas as pl
from jax.experimental.pallas import tpu as pltpu
from jax.sharding import PartitionSpec as P

LAYERS = 6
F = 64
TILE_C = 16
TILE_T = 128
CB = 16
HB = 256
HH = 64
ROWS = HH + HB
PAIRS = (CB + 2 * LAYERS + 2) // 2
LATER = ((64, 320), (64, 320), (64, 320), (64, 320), (80, 320), (96, 320), (128, 320))
EARLIER = ((0, 80), (0, 80), (0, 80), (0, 80), (0, 80), (16, 96), (48, 128))
CHUNK = 16
OWN = ((4, 10), (4, 9))
SLOTS = 32
HIST = 256
EDGE = 16
BF = jnp.bfloat16
F32 = jnp.float32


def split(x):
    hi = x.astype(BF)
    return hi, (x - hi.astype(F32)).astype(BF)


def from_behind(block, axis):
    count = lax.axis_size(axis)
    return lax.ppermute(block, axis, [(i, (i + 1) % count) for i in range(count)])


def exchange(block, axis, first):
    count = lax.axis_size(axis)
    swaps = [(i, (i + 1) % count) for i in range(first, count, 2)]
    return lax.ppermute(block, axis, [p for i, j in swaps for p in ((i, j), (j, i))])


def encoder_weights(small_ref, enc_ref, wide):
    ew = small_ref[0:9] * 0.5
    wide[...] = jnp.zeros(wide.shape, F32)
    for j in range(4):
        for a in range(3):
            for b in range(3):
                wide[b, 3 + 2 * j + a : 4 + 2 * j + a, j * F : j * F + F] = ew[3 * a + b : 3 * a + b + 1, :]
    none = jnp.zeros((F, 256), F32)
    for g in range(8):
        parts = []
        for b in range(3):
            piece = wide[b]
            if g < 7:
                rows = [none[: 8 * g], piece, none[: F - 16 - 8 * g]]
            else:
                rows = [none[: F - 8], piece[:8]]
            parts += [r for r in rows if r.shape[0]]
        parts.append(none)
        enc_ref[g, 0], enc_ref[g, 1] = split(jnp.concatenate(parts, 0))


def layer_weights(layer, dw_ref, dil_ref):
    zero = jnp.zeros((F, F), F32)
    ins = (1, 0, 3, 2) if layer % 2 else (0, 1, 2, 3)
    outs = (1, 2) if layer % 2 else (2, 1)
    rows = []
    for lag in range(2):
        for co in outs:
            cols = [
                dw_ref[layer, 2 * (ci - co + 1) + lag] * 0.5 if 0 <= ci - co + 1 <= 2 else zero
                for ci in ins
            ]
            rows.append(jnp.concatenate(cols, 1))
    dil_ref[layer, 0], dil_ref[layer, 1] = split(jnp.concatenate(rows, 0).T)


def decoder_weights(de, dec_ref, wide):
    wide[...] = jnp.zeros(wide.shape, F32)
    for c in range(CB + 1):
        for a in range(3):
            p = 2 * c + a - 1
            if 0 <= p < 2 * CB:
                for b in range(3):
                    k, at = c % 4 * F, b * 2 * CB + p
                    wide[c // 4, at : at + 1, k : k + F] = de[3 * a + b : 3 * a + b + 1, :]
    for q in range(5):
        hi, lo = split(wide[q].T)
        dec_ref[q] = jnp.concatenate([hi, lo], 1)


def edge_masks(mask):
    m_low = jnp.where(lax.axis_index("fiber") == 0, 0.0, 1.0).astype(F32)
    m_high = jnp.where(lax.axis_index("fiber") == lax.axis_size("fiber") - 1, 0.0, 1.0).astype(F32)
    pair = lax.broadcasted_iota(jnp.int32, (16, 128), 0)
    lane = lax.broadcasted_iota(jnp.int32, (16, 128), 1)
    for layer in range(LAYERS + 1):
        second = lane // F if layer % 2 == 0 else 1 - lane // F
        c = layer - LAYERS + 2 * pair + second
        mask[layer] = jnp.where(c < 0, m_low, jnp.where(c >= CB, m_high, 1.0))


def gather_taps(s, st, first, begin, count, parts, groups):
    both = jnp.concatenate([s, pltpu.roll(s, 1, 1)], 0)
    for n in range(s.shape[1] // 128):
        st[pl.ds(first + n * 128, 128), :] = both[:, n * 128 : n * 128 + 128].T
    x = [st[pl.ds(HIST + 2 * (begin - HH) - back, count, 2), :] for back in (0, 2)]
    for g in range(groups):
        rolled = [pltpu.roll(half, 128 - 8 * g, 1) if g else half for half in x]
        parts[g, 0, begin : begin + count], parts[g, 1, begin : begin + count] = split(jnp.concatenate(rolled, 1))


def network(ranges, parts, hid, top, low, mask, bias, enc_ref, dil_ref, dec_ref, plan, group, ahead, kept, finished):
    eb = bias[0:1]
    low_half = lax.broadcasted_iota(jnp.int32, (1, 128), 1) < F
    m_time = jnp.where(lax.axis_index("tm") == 0, 0.0, 1.0).astype(F32)

    def keep(buf, i, value, layer):
        start, end = ranges[layer]
        if mask is not None:
            value = value * mask[layer, i : i + 1, :]
        if start < HH:
            value = jnp.concatenate([value[: HH - start] * m_time, value[HH - start :]], 0)
        hid[buf, i, start:end] = value
        top[buf, i, start:end], low[buf, i, start:end] = split(value)
        kept(layer, i, value)

    def chunks(pairs, begin, end):
        units = [(i, r) for i in pairs for r in range(begin, end, CHUNK)]
        half = (len(units) + 1) // 2
        return units[:half], units[half:]

    def multiply(acc, units, piece, steps):
        for step, weights in enumerate(steps):
            for n in range(2):
                for k, matrix in enumerate(weights):
                    pltpu.matmul_push_rhs(matrix, k, n)
            for part, load in ((0, 0), (1, None), (0, 1))[: len(weights) + 1]:
                for n in range(2):
                    for slot, unit in enumerate(units[n]):
                        pltpu.matmul_acc_lhs(acc[n][slot], piece(part, step, unit), load if slot == 0 else None)

    def take(acc, units, i):
        out = [pltpu.matmul_pop(acc[n][slot]) for n in range(2) for slot, unit in enumerate(units[n]) if unit[0] == i]
        return jnp.concatenate(out, 0)

    def encode(groups):
        units = chunks(groups, *ranges[0])

        def mm(acc):
            g, same = (0, parts.shape[0] == 1) if len(groups) > 1 else (groups[0], True)
            multiply(acc, units, lambda part, step, unit: parts[0 if same else unit[0], part, unit[1] : unit[1] + CHUNK],
                     ((enc_ref[g, 0], enc_ref[g, 1]),))

        def finish(acc):
            for g in groups:
                y = take(acc, units, g)
                for n in range(2):
                    if 2 * g + n < PAIRS:
                        u = y[:, n * 128 : n * 128 + 128] + eb
                        keep(0, 2 * g + n, u + u * jnp.tanh(u), 0)

        return mm, finish

    def dilated(layer, pairs):
        d = 2**layer
        src, dst = layer % 2, 1 - layer % 2
        start, end = ranges[layer + 1]
        begin = max(ranges[layer][0], (start - d) // CHUNK * CHUNK)
        units = chunks(pairs, begin, end)

        def piece(part, step, unit):
            i, r = unit
            ref = low if part else top
            return jnp.concatenate([ref[src, i, r : r + CHUNK], ref[src, i + 1, r : r + CHUNK]], 1)

        def mm(acc):
            multiply(acc, units, piece, ((dil_ref[layer, 0], dil_ref[layer, 1]),))

        def finish(acc):
            for i in pairs:
                y = take(acc, units, i)
                past = pltpu.roll(y[:, 128:], d, 0)[start - begin :]
                u = y[start - begin :, :128] + past + bias[layer + 1 : layer + 2]
                near, far = (i, i + 1) if src else (i + 1, i)
                h = jnp.where(low_half, hid[src, near, start:end], hid[src, far, start:end])
                keep(dst, i, h + u + u * jnp.tanh(u), layer + 1)

        return mm, finish

    def decode():
        units = chunks((0,), *ranges[LAYERS])

        def piece(part, step, unit):
            ref, r = low if part else top, unit[1]
            return jnp.concatenate([ref[0, i, r : r + CHUNK] for i in (2 * step, min(2 * step + 1, 8))], 1)

        def mm(acc):
            multiply(acc, units, piece, [(dec_ref[q],) for q in range(5)])

        def finish(acc):
            y = take(acc, units, 0)
            finished(y[:, :128] + y[:, 128:])

        return mm, finish

    tasks = [encode(groups) for groups in plan[0]]
    for layer, pairs in enumerate(plan[1:]):
        tasks += [dilated(layer, pairs[i : i + group]) for i in range(0, len(pairs), group)]
        tasks.append(lambda layer=layer: ahead(layer))
    if len(plan) > LAYERS:
        tasks.append(decode())

    def run(*refs):
        sets = [[refs[(2 * s + n) * SLOTS : (2 * s + n + 1) * SLOTS] for n in range(2)] for s in range(2)]
        waiting, turn = None, 0
        for task in tasks:
            if callable(task):
                task()
                continue
            if len(plan) > LAYERS and task is tasks[-1] and waiting:
                waiting()
                waiting = None
            mm, finish = task
            mm(sets[turn])
            if waiting:
                waiting()
            waiting = functools.partial(finish, sets[turn])
            turn = 1 - turn
        waiting()

    pl.run_scoped(run, *[pltpu.ACC(n)((CHUNK, 256), F32) for s in range(2) for n in range(2) for k in range(SLOTS)])


def all_pairs(layer):
    return tuple(range(PAIRS - 1 - layer))


def own(sig_ref, small_ref, dw_ref, enc_ref, h0_ref, h1_ref, st, hid, top, low, parts, dil_ref):
    small = small_ref[...]
    bias = jnp.concatenate([small[18:25], small[18:25]], 1) * 0.5
    layer_weights(0, dw_ref, dil_ref)
    st[HIST - 8 : HIST, :] = jnp.zeros((8, 128), F32)
    none = jnp.zeros((EDGE, 2 * HB), F32)
    gather_taps(jnp.concatenate([none, sig_ref[...], none], 0), st, HIST, HH, HB, parts, 1)

    def kept(layer, i, value):
        if layer == 1:
            h1_ref[i - OWN[1][0]] = value
        elif i in (OWN[0][0], OWN[0][1] - 1):
            h0_ref[0 if i == OWN[0][0] else 1] = value

    plan = (tuple((g,) for g in range(OWN[0][0] // 2, OWN[0][1] // 2)), tuple(range(*OWN[1])))
    network(LATER, parts, hid, top, low, None, bias, enc_ref, dil_ref, None, plan, 2, lambda layer: None, kept, None)


def later(s_ref, small_ref, dw_ref, enc_ref, h0_ref, h1_ref, sums_ref, h4_ref, h5_ref, dil_ref, dec_ref, st, hid, top, low, mask, parts, wide):
    small = small_ref[...]
    bias = jnp.concatenate([small[18:25], small[18:25]], 1) * 0.5
    layer_weights(0, dw_ref, dil_ref)
    edge_masks(mask)
    st[HIST - 8 : HIST, :] = jnp.zeros((8, 128), F32)
    gather_taps(s_ref[...], st, HIST, HH, HB, parts, 1)
    done = [(0, OWN[0][0], h0_ref, 0), (0, OWN[0][1] - 1, h0_ref, 1)]
    done += [(1, i, h1_ref, i - OWN[1][0]) for i in range(*OWN[1])]
    for layer, i, ref, k in done:
        rows = slice(*LATER[layer])
        value = ref[k]
        hid[layer, i, rows] = value
        top[layer, i, rows], low[layer, i, rows] = split(value)
    plan = [[(g,) for g in range(8) if not OWN[0][0] <= 2 * g < OWN[0][1]]]
    plan += [all_pairs(layer) for layer in range(LAYERS)]
    plan[1] = tuple(i for i in plan[1] if not OWN[1][0] <= i < OWN[1][1])

    def ahead(layer):
        if layer + 1 < LAYERS:
            layer_weights(layer + 1, dw_ref, dil_ref)
        if layer == 2:
            decoder_weights(small[9:18], dec_ref, wide)

    def kept(layer, i, value):
        if layer == 4:
            h4_ref[i] = value[:16]
        if layer == 5:
            h5_ref[i] = value[:32]

    def finished(sums):
        sums_ref[...] = sums

    network(LATER, parts, hid, top, low, mask, bias, enc_ref, dil_ref, dec_ref, plan, 2, ahead, kept, finished)


def earlier(s_ref, hist_ref, small_ref, enc_ref, sums_ref, h4_ref, h5_ref, dil_ref, dec_ref,
            recon_ref, err_ref, st, hid, top, low, mask, parts, wide, whole):
    small = small_ref[...]
    bias = jnp.concatenate([small[18:25], small[18:25]], 1) * 0.5
    edge_masks(mask)
    hist = jnp.where(lax.axis_index("tm") == 0, 0.0, hist_ref[...])
    gather_taps(jnp.concatenate([hist, s_ref[:, :128]], 1), st, 0, 0, EARLIER[0][1], parts, 8)
    for buf, ref, begin, end in ((0, h4_ref, 80, 96), (1, h5_ref, 96, 128)):
        for i in range(ref.shape[0]):
            value = ref[i]
            hid[buf, i, begin:end] = value
            top[buf, i, begin:end], low[buf, i, begin:end] = split(value)

    base = EARLIER[LAYERS][0]
    whole[EARLIER[LAYERS][1] - base :, :] = sums_ref[...]

    def scores(tiles):
        begin, count = HH - base + tiles[0] * TILE_T // 2, len(tiles) * TILE_T // 2
        now, past = whole[begin : begin + count, :], whole[begin - 1 : begin - 1 + count, :]
        wide[pl.ds(tiles[0] * TILE_T, count, 2), :] = now + pltpu.roll(past, 128 - 4 * CB, 1)
        wide[pl.ds(tiles[0] * TILE_T + 1, count, 2), :] = pltpu.roll(now, 128 - 2 * CB, 1)
        for n in tiles:
            cols = slice(n * TILE_T, n * TILE_T + TILE_T)
            out = wide[cols, :].T[: 2 * CB]
            recon_ref[:, cols] = out
            sq = (out - s_ref[EDGE : EDGE + 2 * CB, cols]) ** 2
            per = [jnp.sum(sq[m * TILE_C : m * TILE_C + TILE_C], keepdims=True) for m in range(2 * CB // TILE_C)]
            err_ref[:, n : n + 1] = jnp.concatenate(per, 0) * (1.0 / (TILE_C * TILE_T))

    def ahead(layer):
        if layer == 1:
            scores((2, 3))

    def finished(value):
        whole[: EARLIER[LAYERS][1] - base, :] = value

    plan = [[tuple(range(4)), tuple(range(4, 8))]] + [all_pairs(layer) for layer in range(LAYERS)]
    network(EARLIER, parts, hid, top, low, mask, bias, enc_ref, dil_ref, dec_ref, plan, 4, ahead,
            lambda layer, i, value: None, finished)
    scores((0, 1))


def on_device(signal, encode_weight, encode_bias, dilated_weight, dilated_bias, decode_weight):
    vmem = pl.BlockSpec(memory_space=pltpu.VMEM)
    far = exchange(signal, "fiber", 1)
    small = jnp.concatenate(
        [encode_weight.T, decode_weight, encode_bias.reshape(1, F), dilated_bias], 0
    )
    signal, small = lax.optimization_barrier((signal, small))
    near = exchange(signal, "fiber", 0)
    enc = pl.pallas_call(
        encoder_weights,
        out_shape=jax.ShapeDtypeStruct((8, 2, 256, 256), BF),
        in_specs=[vmem],
        out_specs=vmem,
        scratch_shapes=[pltpu.VMEM((3, 16, 256), F32)],
        cost_estimate=pl.CostEstimate(flops=10**6, bytes_accessed=2 * 10**6, transcendentals=0),
        compiler_params=pltpu.CompilerParams(vmem_limit_bytes=16 * 2**20),
        name="encoder_weights",
    )(small)
    scratch = [
        pltpu.VMEM((HIST + 2 * HB, 128), F32),
        pltpu.VMEM((2, 16, ROWS, 128), F32),
        pltpu.VMEM((2, 16, ROWS, 128), BF),
        pltpu.VMEM((2, 16, ROWS, 128), BF),
    ]
    params = pltpu.CompilerParams(vmem_limit_bytes=32 * 2**20)
    h0, h1 = pl.pallas_call(
        own,
        out_shape=(
            jax.ShapeDtypeStruct((2, HB, 128), F32),
            jax.ShapeDtypeStruct((OWN[1][1] - OWN[1][0], HB, 128), F32),
        ),
        in_specs=[vmem] * 4,
        out_specs=(vmem,) * 2,
        scratch_shapes=scratch + [pltpu.VMEM((1, 2, ROWS, 256), BF), pltpu.VMEM((1, 2, 256, 256), BF)],
        cost_estimate=pl.CostEstimate(flops=10**9, bytes_accessed=2 * 10**6, transcendentals=0),
        compiler_params=params,
        name="own",
    )(signal, small, dilated_weight, enc)
    near, far, h0, h1 = lax.optimization_barrier((near, far, h0, h1))
    even = lax.axis_index("fiber") % 2 == 0
    first = lax.axis_index("fiber") == 0
    last = lax.axis_index("fiber") == lax.axis_size("fiber") - 1
    below = jnp.where(first, 0.0, jnp.where(even, far[2 * CB - EDGE :], near[2 * CB - EDGE :]))
    above = jnp.where(last, 0.0, jnp.where(even, near[:EDGE], far[:EDGE]))
    section = jnp.concatenate([below, signal, above], 0)
    history = from_behind(section[:, 2 * HB - HIST :], "tm")
    scratch = scratch + [pltpu.VMEM((LAYERS + 1, 16, 128), F32)]
    sums, h4, h5, dil, dec = pl.pallas_call(
        later,
        out_shape=(
            jax.ShapeDtypeStruct((LATER[LAYERS][1] - LATER[LAYERS][0], 128), F32),
            jax.ShapeDtypeStruct((PAIRS - 4, 16, 128), F32),
            jax.ShapeDtypeStruct((PAIRS - 5, 32, 128), F32),
            jax.ShapeDtypeStruct((LAYERS, 2, 256, 256), BF),
            jax.ShapeDtypeStruct((5, 256, 256), BF),
        ),
        in_specs=[vmem] * 6,
        out_specs=(vmem,) * 5,
        scratch_shapes=scratch + [pltpu.VMEM((1, 2, ROWS, 256), BF), pltpu.VMEM((5, 128, 256), F32)],
        cost_estimate=pl.CostEstimate(flops=8 * 10**9, bytes_accessed=8 * 10**6, transcendentals=0),
        compiler_params=params,
        name="later",
    )(section, small, dilated_weight, enc, h0, h1)
    return pl.pallas_call(
        earlier,
        out_shape=(
            jax.ShapeDtypeStruct((2 * CB, 2 * HB), F32),
            jax.ShapeDtypeStruct((2 * CB // TILE_C, 2 * HB // TILE_T), F32),
        ),
        in_specs=[vmem] * 9,
        out_specs=(vmem,) * 2,
        scratch_shapes=scratch
        + [pltpu.VMEM((8, 2, EARLIER[0][1], 256), BF), pltpu.VMEM((2 * HB, 128), F32), pltpu.VMEM((ROWS - EARLIER[LAYERS][0], 128), F32)],
        cost_estimate=pl.CostEstimate(flops=2 * 10**9, bytes_accessed=8 * 10**6, transcendentals=0),
        compiler_params=params,
        name="earlier",
    )(section, history, small, enc, sums, h4, h5, dil, dec)


def solution(mesh):
    return jax.shard_map(
        on_device,
        mesh=mesh,
        in_specs=(P("fiber", "tm"), P(), P(), P(), P(), P()),
        out_specs=(P("fiber", "tm"), P("fiber", "tm")),
        check_vma=False,
    )
```

```python
import functools

import jax
import jax.numpy as jnp
from jax import lax
from jax.experimental import pallas as pl
from jax.experimental.pallas import tpu as pltpu
from jax.sharding import PartitionSpec as P

LAYERS = 6
F = 64
TILE_C = 16
TILE_T = 128
CB = 16
HB = 256
HH = 64
ROWS = HH + HB
PAIRS = (CB + 2 * LAYERS + 2) // 2
LATER = ((64, 320), (64, 320), (64, 320), (64, 320), (80, 320), (96, 320), (128, 320))
EARLIER = ((0, 80), (0, 80), (0, 80), (0, 80), (0, 80), (16, 96), (48, 128))
CHUNK = 16
OWN = ((4, 10), (4, 9), (4, 8))
SLOTS = 32
HIST = 256
EDGE = 16
BF = jnp.bfloat16
F32 = jnp.float32


def split(x):
    hi = x.astype(BF)
    return hi, (x - hi.astype(F32)).astype(BF)


def from_behind(block, axis):
    count = lax.axis_size(axis)
    return lax.ppermute(block, axis, [(i, (i + 1) % count) for i in range(count)])


def exchange(block, first):
    times, count = lax.axis_size("tm"), lax.axis_size("fiber")
    swaps = [(t * count + i, t * count + i + 1) for t in range(times) for i in range(first, count - 1, 2)]
    if first:
        swaps += [(t * count + i, (t + 1) * count + i) for t in range(0, times, 2) for i in (0, count - 1)]
    return lax.ppermute(block, ("tm", "fiber"), [p for i, j in swaps for p in ((i, j), (j, i))])


def encoder_weights(small_ref, enc_ref, wide):
    ew = small_ref[0:9] * 0.5
    wide[...] = jnp.zeros(wide.shape, F32)
    for j in range(4):
        for a in range(3):
            for b in range(3):
                wide[b, 3 + 2 * j + a : 4 + 2 * j + a, j * F : j * F + F] = ew[3 * a + b : 3 * a + b + 1, :]
    none = jnp.zeros((F, 256), F32)
    for g in range(8):
        parts = []
        for b in range(3):
            piece = wide[b]
            if g < 7:
                rows = [none[: 8 * g], piece, none[: F - 16 - 8 * g]]
            else:
                rows = [none[: F - 8], piece[:8]]
            parts += [r for r in rows if r.shape[0]]
        parts.append(none)
        enc_ref[g, 0], enc_ref[g, 1] = split(jnp.concatenate(parts, 0))


def layer_weights(layer, dw_ref, dil_ref):
    zero = jnp.zeros((F, F), F32)
    ins = (1, 0, 3, 2) if layer % 2 else (0, 1, 2, 3)
    outs = (1, 2) if layer % 2 else (2, 1)
    rows = []
    for lag in range(2):
        for co in outs:
            cols = [
                dw_ref[layer, 2 * (ci - co + 1) + lag] * 0.5 if 0 <= ci - co + 1 <= 2 else zero
                for ci in ins
            ]
            rows.append(jnp.concatenate(cols, 1))
    dil_ref[layer, 0], dil_ref[layer, 1] = split(jnp.concatenate(rows, 0).T)


def decoder_weights(de, dec_ref, wide):
    wide[...] = jnp.zeros(wide.shape, F32)
    for c in range(CB + 1):
        for a in range(3):
            p = 2 * c + a - 1
            if 0 <= p < 2 * CB:
                for b in range(3):
                    k, at = c % 4 * F, b * 2 * CB + p
                    wide[c // 4, at : at + 1, k : k + F] = de[3 * a + b : 3 * a + b + 1, :]
    for q in range(5):
        hi, lo = split(wide[q].T)
        dec_ref[q] = jnp.concatenate([hi, lo], 1)


def edge_masks(mask):
    m_low = jnp.where(lax.axis_index("fiber") == 0, 0.0, 1.0).astype(F32)
    m_high = jnp.where(lax.axis_index("fiber") == lax.axis_size("fiber") - 1, 0.0, 1.0).astype(F32)
    pair = lax.broadcasted_iota(jnp.int32, (16, 128), 0)
    lane = lax.broadcasted_iota(jnp.int32, (16, 128), 1)
    for layer in range(LAYERS + 1):
        second = lane // F if layer % 2 == 0 else 1 - lane // F
        c = layer - LAYERS + 2 * pair + second
        mask[layer] = jnp.where(c < 0, m_low, jnp.where(c >= CB, m_high, 1.0))


def gather_taps(s, st, first, begin, count, parts, groups):
    both = jnp.concatenate([s, pltpu.roll(s, 1, 1)], 0)
    for n in range(s.shape[1] // 128):
        st[pl.ds(first + n * 128, 128), :] = both[:, n * 128 : n * 128 + 128].T
    x = [st[pl.ds(HIST + 2 * (begin - HH) - back, count, 2), :] for back in (0, 2)]
    for g in range(groups):
        rolled = [pltpu.roll(half, 128 - 8 * g, 1) if g else half for half in x]
        parts[g, 0, begin : begin + count], parts[g, 1, begin : begin + count] = split(jnp.concatenate(rolled, 1))


def network(tasks_of, parts, hid, top, low, mask, bias, enc_ref, dil_ref, dec_ref, kept):
    eb = bias[0:1]
    low_half = lax.broadcasted_iota(jnp.int32, (1, 128), 1) < F
    sublane = lax.broadcasted_iota(jnp.int32, (8, 128), 0)
    m_time = jnp.where(lax.axis_index("tm") == 0, 0.0, 1.0).astype(F32)

    def keep(buf, i, value, layer, r, scale):
        if scale is not None:
            value = value * scale
        if r < HH:
            value = value * m_time
        hid[buf, i, r : r + CHUNK] = value
        top[buf, i, r : r + CHUNK], low[buf, i, r : r + CHUNK] = split(value)
        kept(layer, i, value, r)

    def scale_of(layer, i):
        return None if mask is None else mask[layer, i : i + 1, :]

    def chunks(pairs, begin, end):
        units = [(i, r) for i in pairs for r in range(begin, end, CHUNK)]
        half = (len(units) + 1) // 2
        return units[:half], units[half:]

    def multiply(acc, units, piece, steps):
        for step, weights in enumerate(steps):
            for n in range(2):
                for k, matrix in enumerate(weights):
                    pltpu.matmul_push_rhs(matrix, k, n)
            for part, load in ((0, 0), (1, None), (0, 1))[: len(weights) + 1]:
                for n in range(2):
                    for slot, unit in enumerate(units[n]):
                        pltpu.matmul_acc_lhs(acc[n][slot], piece(part, step, unit), load if slot == 0 else None)

    def each(acc, units, i):
        for n in range(2):
            for slot, unit in enumerate(units[n]):
                if unit[0] == i:
                    yield unit[1], pltpu.matmul_pop(acc[n][slot])

    def encode(ranges, groups):
        units = chunks(groups, *ranges[0])

        def mm(acc):
            g, same = (0, parts.shape[0] == 1) if len(groups) > 1 else (groups[0], True)
            multiply(acc, units, lambda part, step, unit: parts[0 if same else unit[0], part, unit[1] : unit[1] + CHUNK],
                     ((enc_ref[g, 0], enc_ref[g, 1]),))

        def finish(acc):
            for g in groups:
                scales = [scale_of(0, 2 * g + n) for n in range(2)]
                for r, y in each(acc, units, g):
                    for n in range(2):
                        if 2 * g + n < PAIRS:
                            u = y[:, n * 128 : n * 128 + 128] + eb
                            keep(0, 2 * g + n, u + u * jnp.tanh(u), 0, r, scales[n])

        return mm, finish

    def dilated(ranges, layer, pairs):
        d = 2**layer
        src, dst = layer % 2, 1 - layer % 2
        start, end = ranges[layer + 1]
        begin = max(ranges[layer][0], (start - d) // CHUNK * CHUNK)
        units = chunks(pairs, begin, end)

        def piece(part, step, unit):
            i, r = unit
            ref = low if part else top
            return jnp.concatenate([ref[src, i, r : r + CHUNK], ref[src, i + 1, r : r + CHUNK]], 1)

        def mm(acc):
            multiply(acc, units, piece, ((dil_ref[layer, 0], dil_ref[layer, 1]),))

        def finish(acc):
            for i in pairs:
                near, far = (i, i + 1) if src else (i + 1, i)
                scale = scale_of(layer + 1, i)
                lagged = {}
                for r, y in each(acc, units, i):
                    for k in range(0, CHUNK, 8):
                        lagged[r + k] = y[k : k + 8, 128:]
                        if d < 8:
                            lagged[r + k] = pltpu.roll(lagged[r + k], d, 0)
                    if r < start:
                        continue
                    past = []
                    for k in range(r, r + CHUNK, 8):
                        if d < 8:
                            past.append(jnp.where(sublane < d, lagged.get(k - 8, lagged[k]), lagged[k]))
                        else:
                            past.append(lagged.get(k - d, lagged[k]))
                    u = y[:, :128] + jnp.concatenate(past, 0) + bias[layer + 1 : layer + 2]
                    rows = slice(r, r + CHUNK)
                    h = jnp.where(low_half, hid[src, near, rows], hid[src, far, rows])
                    keep(dst, i, h + u + u * jnp.tanh(u), layer + 1, r, scale)

        return mm, finish

    def decode(ranges, finished):
        units = chunks((0,), *ranges[LAYERS])

        def piece(part, step, unit):
            ref, r = low if part else top, unit[1]
            return jnp.concatenate([ref[0, i, r : r + CHUNK] for i in (2 * step, min(2 * step + 1, 8))], 1)

        def mm(acc):
            multiply(acc, units, piece, [(dec_ref[q],) for q in range(5)])

        def finish(acc):
            for r, y in each(acc, units, 0):
                finished(r, y[:, :128] + y[:, 128:])

        return mm, finish

    tasks = tasks_of(encode, dilated, decode)

    def run(*refs):
        sets = [[refs[(2 * s + n) * SLOTS : (2 * s + n + 1) * SLOTS] for n in range(2)] for s in range(2)]
        waiting, turn = None, 0
        for task in tasks:
            if callable(task):
                task()
                continue
            if task is None:
                if waiting:
                    waiting()
                waiting = None
                continue
            mm, finish = task
            mm(sets[turn])
            if waiting:
                waiting()
            waiting = functools.partial(finish, sets[turn])
            turn = 1 - turn
        if waiting:
            waiting()

    pl.run_scoped(run, *[pltpu.ACC(n)((CHUNK, 256), F32) for s in range(2) for n in range(2) for k in range(SLOTS)])


def all_pairs(layer, group):
    pairs = tuple(range(PAIRS - 1 - layer))
    return [pairs[i : i + group] for i in range(0, len(pairs), group)]


def handed(layer):
    pairs = range(*OWN[layer])
    return list(pairs) if layer == len(OWN) - 1 else [pairs[0], pairs[-1]]


def own(sig_ref, small_ref, dw_ref, enc_ref, *refs):
    outs = refs[: len(OWN)]
    st, hid, top, low, parts, dil_ref = refs[len(OWN) :]
    small = small_ref[...]
    bias = jnp.concatenate([small[18:25], small[18:25]], 1) * 0.5
    st[HIST - 8 : HIST, :] = jnp.zeros((8, 128), F32)
    none = jnp.zeros((EDGE, 2 * HB), F32)
    gather_taps(jnp.concatenate([none, sig_ref[...], none], 0), st, HIST, HH, HB, parts, 1)
    for layer in range(len(OWN) - 1):
        layer_weights(layer, dw_ref, dil_ref)

    def kept(layer, i, value, r):
        if i in handed(layer):
            at = r - LATER[layer][0]
            outs[layer][handed(layer).index(i), at : at + CHUNK] = value

    def tasks(encode, dilated, decode):
        out = [encode(LATER, (g,)) for g in range(OWN[0][0] // 2, OWN[0][1] // 2)]
        for layer in range(len(OWN) - 1):
            pairs = tuple(range(*OWN[layer + 1]))
            out += [dilated(LATER, layer, group) for group in (pairs[:2], *zip(pairs[2:]))]
        return out

    network(tasks, parts, hid, top, low, None, bias, enc_ref, dil_ref, None, kept)


def later(s_ref, small_ref, dw_ref, enc_ref, *refs):
    done = refs[: len(OWN)]
    sums_ref, h4_ref, h5_ref, dil_ref, dec_ref, st, hid, top, low, mask, parts, wide = refs[len(OWN) :]
    small = small_ref[...]
    bias = jnp.concatenate([small[18:25], small[18:25]], 1) * 0.5
    layer_weights(0, dw_ref, dil_ref)
    edge_masks(mask)
    st[HIST - 8 : HIST, :] = jnp.zeros((8, 128), F32)
    gather_taps(s_ref[...], st, HIST, HH, HB, parts, 1)

    def fetch(layer):
        rows = slice(*LATER[layer])
        for k, i in enumerate(handed(layer)):
            value = done[layer][k]
            hid[layer % 2, i, rows] = value
            top[layer % 2, i, rows], low[layer % 2, i, rows] = split(value)

    def kept(layer, i, value, r):
        if layer == 4 and r < EARLIER[5][1]:
            h4_ref[i, r - LATER[4][0] : r - LATER[4][0] + CHUNK] = value
        if layer == 5 and r < EARLIER[6][1]:
            h5_ref[i, r - LATER[5][0] : r - LATER[5][0] + CHUNK] = value

    def store(r, value):
        sums_ref[r - LATER[LAYERS][0] : r - LATER[LAYERS][0] + CHUNK, :] = value

    def tasks(encode, dilated, decode):
        out = [functools.partial(fetch, 0), functools.partial(fetch, 1)]
        out += [encode(LATER, (g,)) for g in range(8) if not OWN[0][0] <= 2 * g < OWN[0][1]]
        for layer in range(LAYERS):
            pairs = [i for i in range(PAIRS - 1 - layer) if layer + 1 >= len(OWN) or i not in range(*OWN[layer + 1])]
            out += [dilated(LATER, layer, pairs[i : i + 2]) for i in range(0, len(pairs), 2)]
            if 2 <= layer + 2 < len(OWN):
                out += [None, functools.partial(fetch, layer + 2)]
            if layer + 1 < LAYERS:
                out.append(functools.partial(layer_weights, layer + 1, dw_ref, dil_ref))
            if layer == 2:
                out.append(lambda: decoder_weights(small[9:18], dec_ref, wide))
        return out + [None, decode(LATER, store)]

    network(tasks, parts, hid, top, low, mask, bias, enc_ref, dil_ref, dec_ref, kept)


def earlier(s_ref, hist_ref, small_ref, enc_ref, sums_ref, h4_ref, h5_ref, dil_ref, dec_ref,
            recon_ref, err_ref, st, hid, top, low, mask, parts, wide, whole):
    small = small_ref[...]
    bias = jnp.concatenate([small[18:25], small[18:25]], 1) * 0.5
    edge_masks(mask)
    hist = jnp.where(lax.axis_index("tm") == 0, 0.0, hist_ref[...])
    gather_taps(jnp.concatenate([hist, s_ref[:, :128]], 1), st, 0, 0, EARLIER[0][1], parts, 8)
    base = EARLIER[LAYERS][0]

    def fetch():
        for buf, ref, begin, end in ((0, h4_ref, 80, 96), (1, h5_ref, 96, 128)):
            for i in range(ref.shape[0]):
                value = ref[i]
                hid[buf, i, begin:end] = value
                top[buf, i, begin:end], low[buf, i, begin:end] = split(value)
        whole[LATER[LAYERS][0] - base :, :] = sums_ref[...]

    def scores(tiles):
        begin, count = HH - base + tiles[0] * TILE_T // 2, len(tiles) * TILE_T // 2
        now, past = whole[begin : begin + count, :], whole[begin - 1 : begin - 1 + count, :]
        wide[pl.ds(tiles[0] * TILE_T, count, 2), :] = now + pltpu.roll(past, 128 - 4 * CB, 1)
        wide[pl.ds(tiles[0] * TILE_T + 1, count, 2), :] = pltpu.roll(now, 128 - 2 * CB, 1)
        for n in tiles:
            cols = slice(n * TILE_T, n * TILE_T + TILE_T)
            out = wide[cols, :].T[: 2 * CB]
            recon_ref[:, cols] = out
            sq = (out - s_ref[EDGE : EDGE + 2 * CB, cols]) ** 2
            per = [jnp.sum(sq[m * TILE_C : m * TILE_C + TILE_C], keepdims=True) for m in range(2 * CB // TILE_C)]
            err_ref[:, n : n + 1] = jnp.concatenate(per, 0) * (1.0 / (TILE_C * TILE_T))

    def store(r, value):
        whole[r - base : r - base + CHUNK, :] = value

    def tasks(encode, dilated, decode):
        out = [encode(EARLIER, (0, 1, 2, 3)), encode(EARLIER, (4, 5, 6, 7)), fetch]
        for layer in range(LAYERS):
            out += [dilated(EARLIER, layer, pairs) for pairs in all_pairs(layer, 4)]
            if layer == 1:
                out.append(functools.partial(scores, (2, 3)))
        return out + [None, decode(EARLIER, store)]

    network(tasks, parts, hid, top, low, mask, bias, enc_ref, dil_ref, dec_ref, lambda layer, i, value, r: None)
    scores((0, 1))


def on_device(signal, encode_weight, encode_bias, dilated_weight, dilated_bias, decode_weight):
    vmem = pl.BlockSpec(memory_space=pltpu.VMEM)
    far = exchange(signal, 1)
    small = jnp.concatenate(
        [encode_weight.T, decode_weight, encode_bias.reshape(1, F), dilated_bias], 0
    )
    near = exchange(signal, 0)
    enc = pl.pallas_call(
        encoder_weights,
        out_shape=jax.ShapeDtypeStruct((8, 2, 256, 256), BF),
        in_specs=[vmem],
        out_specs=vmem,
        scratch_shapes=[pltpu.VMEM((3, 16, 256), F32)],
        cost_estimate=pl.CostEstimate(flops=10**6, bytes_accessed=2 * 10**6, transcendentals=0),
        compiler_params=pltpu.CompilerParams(vmem_limit_bytes=16 * 2**20),
        name="encoder_weights",
    )(small)
    scratch = [
        pltpu.VMEM((HIST + 2 * HB, 128), F32),
        pltpu.VMEM((2, 16, ROWS, 128), F32),
        pltpu.VMEM((2, 16, ROWS, 128), BF),
        pltpu.VMEM((2, 16, ROWS, 128), BF),
    ]
    params = pltpu.CompilerParams(vmem_limit_bytes=32 * 2**20)
    done = pl.pallas_call(
        own,
        out_shape=tuple(jax.ShapeDtypeStruct((len(handed(layer)), HB, 128), F32) for layer in range(len(OWN))),
        in_specs=[vmem] * 4,
        out_specs=(vmem,) * len(OWN),
        scratch_shapes=scratch
        + [pltpu.VMEM((1, 2, ROWS, 256), BF), pltpu.VMEM((len(OWN) - 1, 2, 256, 256), BF)],
        cost_estimate=pl.CostEstimate(flops=10**9, bytes_accessed=2 * 10**6, transcendentals=0),
        compiler_params=params,
        name="own",
    )(signal, small, dilated_weight, enc)
    near, far, *done = lax.optimization_barrier((near, far, *done))
    even = lax.axis_index("fiber") % 2 == 0
    first = lax.axis_index("fiber") == 0
    last = lax.axis_index("fiber") == lax.axis_size("fiber") - 1
    below = jnp.where(first, 0.0, jnp.where(even, far[2 * CB - EDGE :], near[2 * CB - EDGE :]))
    above = jnp.where(last, 0.0, jnp.where(even, near[:EDGE], far[:EDGE]))
    section = jnp.concatenate([below, signal, above], 0)
    history = from_behind(section[:, 2 * HB - HIST :], "tm")
    scratch = scratch + [pltpu.VMEM((LAYERS + 1, 16, 128), F32)]
    results = pl.pallas_call(
        later,
        out_shape=(
            jax.ShapeDtypeStruct((LATER[LAYERS][1] - LATER[LAYERS][0], 128), F32),
            jax.ShapeDtypeStruct((PAIRS - 4, EARLIER[5][1] - LATER[4][0], 128), F32),
            jax.ShapeDtypeStruct((PAIRS - 5, EARLIER[6][1] - LATER[5][0], 128), F32),
            jax.ShapeDtypeStruct((LAYERS, 2, 256, 256), BF),
            jax.ShapeDtypeStruct((5, 256, 256), BF),
        ),
        in_specs=[vmem] * (4 + len(OWN)),
        out_specs=(vmem,) * 5,
        scratch_shapes=scratch + [pltpu.VMEM((1, 2, ROWS, 256), BF), pltpu.VMEM((5, 128, 256), F32)],
        cost_estimate=pl.CostEstimate(flops=7 * 10**9, bytes_accessed=8 * 10**6, transcendentals=0),
        compiler_params=params,
        name="later",
    )(section, small, dilated_weight, enc, *done)
    return pl.pallas_call(
        earlier,
        out_shape=(
            jax.ShapeDtypeStruct((2 * CB, 2 * HB), F32),
            jax.ShapeDtypeStruct((2 * CB // TILE_C, 2 * HB // TILE_T), F32),
        ),
        in_specs=[vmem] * 9,
        out_specs=(vmem,) * 2,
        scratch_shapes=scratch
        + [
            pltpu.VMEM((8, 2, EARLIER[0][1], 256), BF),
            pltpu.VMEM((2 * HB, 128), F32),
            pltpu.VMEM((ROWS - EARLIER[LAYERS][0], 128), F32),
        ],
        cost_estimate=pl.CostEstimate(flops=2 * 10**9, bytes_accessed=8 * 10**6, transcendentals=0),
        compiler_params=params,
        name="earlier",
    )(section, history, small, enc, *results)


def solution(mesh):
    return jax.shard_map(
        on_device,
        mesh=mesh,
        in_specs=(P("fiber", "tm"), P(), P(), P(), P(), P()),
        out_specs=(P("fiber", "tm"), P("fiber", "tm")),
        check_vma=False,
    )
```

```python
import functools

import jax
import jax.numpy as jnp
from jax import lax
from jax.experimental import pallas as pl
from jax.experimental.pallas import tpu as pltpu
from jax.sharding import PartitionSpec as P

LAYERS = 6
F = 64
TILE_C = 16
TILE_T = 128
CB = 16
HB = 256
HH = 64
ROWS = HH + HB
PAIRS = (CB + 2 * LAYERS + 2) // 2
LATER = ((64, 320), (64, 320), (64, 320), (64, 320), (80, 320), (96, 320), (128, 320))
EARLIER = ((0, 80), (0, 80), (0, 80), (0, 80), (0, 80), (16, 96), (48, 128))
CHUNK = 16
OWN = ((4, 10), (4, 9), (4, 8))
SLOTS = 32
HIST = 256
EDGE = 16
BF = jnp.bfloat16
F32 = jnp.float32


def split(x):
    hi = x.astype(BF)
    return hi, (x - hi.astype(F32)).astype(BF)


def from_behind(block, axis):
    count = lax.axis_size(axis)
    return lax.ppermute(block, axis, [(i, (i + 1) % count) for i in range(count)])


def exchange(block, first):
    times, count = lax.axis_size("tm"), lax.axis_size("fiber")
    swaps = [(t * count + i, t * count + i + 1) for t in range(times) for i in range(first, count - 1, 2)]
    if first:
        swaps += [(t * count + i, (t + 1) * count + i) for t in range(0, times, 2) for i in (0, count - 1)]
    return lax.ppermute(block, ("tm", "fiber"), [p for i, j in swaps for p in ((i, j), (j, i))])


def encoder_weights(small_ref, enc_ref, wide):
    ew = small_ref[0:9] * 0.5
    wide[...] = jnp.zeros(wide.shape, F32)
    for j in range(4):
        for a in range(3):
            for b in range(3):
                wide[b, 3 + 2 * j + a : 4 + 2 * j + a, j * F : j * F + F] = ew[3 * a + b : 3 * a + b + 1, :]
    none = jnp.zeros((F, 256), F32)
    for g in range(8):
        parts = []
        for b in range(3):
            piece = wide[b]
            if g < 7:
                rows = [none[: 8 * g], piece, none[: F - 16 - 8 * g]]
            else:
                rows = [none[: F - 8], piece[:8]]
            parts += [r for r in rows if r.shape[0]]
        parts.append(none)
        enc_ref[g, 0], enc_ref[g, 1] = split(jnp.concatenate(parts, 0))


def layer_weights(layer, dw_ref, dil_ref):
    zero = jnp.zeros((F, F), F32)
    ins = (1, 0, 3, 2) if layer % 2 else (0, 1, 2, 3)
    outs = (1, 2) if layer % 2 else (2, 1)
    rows = []
    for lag in range(2):
        for co in outs:
            cols = [
                dw_ref[layer, 2 * (ci - co + 1) + lag] * 0.5 if 0 <= ci - co + 1 <= 2 else zero
                for ci in ins
            ]
            rows.append(jnp.concatenate(cols, 1))
    dil_ref[layer, 0], dil_ref[layer, 1] = split(jnp.concatenate(rows, 0).T)


def decoder_weights(de, dec_ref, wide):
    wide[...] = jnp.zeros(wide.shape, F32)
    for c in range(CB + 1):
        for a in range(3):
            p = 2 * c + a - 1
            if 0 <= p < 2 * CB:
                for b in range(3):
                    k, at = c % 4 * F, b * 2 * CB + p
                    wide[c // 4, at : at + 1, k : k + F] = de[3 * a + b : 3 * a + b + 1, :]
    for q in range(5):
        hi, lo = split(wide[q].T)
        dec_ref[q] = jnp.concatenate([hi, lo], 1)


def edge_masks(mask):
    m_low = jnp.where(lax.axis_index("fiber") == 0, 0.0, 1.0).astype(F32)
    m_high = jnp.where(lax.axis_index("fiber") == lax.axis_size("fiber") - 1, 0.0, 1.0).astype(F32)
    pair = lax.broadcasted_iota(jnp.int32, (16, 128), 0)
    lane = lax.broadcasted_iota(jnp.int32, (16, 128), 1)
    for layer in range(LAYERS + 1):
        second = lane // F if layer % 2 == 0 else 1 - lane // F
        c = layer - LAYERS + 2 * pair + second
        mask[layer] = jnp.where(c < 0, m_low, jnp.where(c >= CB, m_high, 1.0))


def gather_taps(s, st, first, begin, count, parts, groups):
    both = jnp.concatenate([s, pltpu.roll(s, 1, 1)], 0)
    for n in range(s.shape[1] // 128):
        st[pl.ds(first + n * 128, 128), :] = both[:, n * 128 : n * 128 + 128].T
    x = [st[pl.ds(HIST + 2 * (begin - HH) - back, count, 2), :] for back in (0, 2)]
    for g in range(groups):
        rolled = [pltpu.roll(half, 128 - 8 * g, 1) if g else half for half in x]
        parts[g, 0, begin : begin + count], parts[g, 1, begin : begin + count] = split(jnp.concatenate(rolled, 1))


def network(tasks_of, parts, hid, top, low, mask, bias, enc_ref, dil_ref, dec_ref, kept):
    eb = bias[0:1]
    low_half = lax.broadcasted_iota(jnp.int32, (1, 128), 1) < F
    sublane = lax.broadcasted_iota(jnp.int32, (8, 128), 0)
    m_time = jnp.where(lax.axis_index("tm") == 0, 0.0, 1.0).astype(F32)

    def keep(buf, i, value, layer, r, scale):
        if scale is not None:
            value = value * scale
        if r < HH:
            value = value * m_time
        hid[buf, i, r : r + CHUNK] = value
        top[buf, i, r : r + CHUNK], low[buf, i, r : r + CHUNK] = split(value)
        kept(layer, i, value, r)

    def scale_of(layer, i):
        c = layer - LAYERS + 2 * i
        return None if mask is None or 0 <= c < CB - 1 else mask[layer, i : i + 1, :]

    def chunks(pairs, begin, end):
        units = [(i, r) for i in pairs for r in range(begin, end, CHUNK)]
        half = (len(units) + 1) // 2
        return units[:half], units[half:]

    def multiply(acc, units, piece, steps):
        for step, weights in enumerate(steps):
            for n in range(2):
                for k, matrix in enumerate(weights):
                    pltpu.matmul_push_rhs(matrix, k, n)
            for part, load in ((0, 0), (1, None), (0, 1))[: len(weights) + 1]:
                for n in range(2):
                    for slot, unit in enumerate(units[n]):
                        pltpu.matmul_acc_lhs(acc[n][slot], piece(part, step, unit), load if slot == 0 else None)

    def each(acc, units, i):
        for n in range(2):
            for slot, unit in enumerate(units[n]):
                if unit[0] == i:
                    yield unit[1], pltpu.matmul_pop(acc[n][slot])

    def encode(ranges, groups):
        units = chunks(groups, *ranges[0])

        def mm(acc):
            g, same = (0, parts.shape[0] == 1) if len(groups) > 1 else (groups[0], True)
            multiply(acc, units, lambda part, step, unit: parts[0 if same else unit[0], part, unit[1] : unit[1] + CHUNK],
                     ((enc_ref[g, 0], enc_ref[g, 1]),))

        def finish(acc):
            for g in groups:
                scales = [scale_of(0, 2 * g + n) for n in range(2)]
                for r, y in each(acc, units, g):
                    for n in range(2):
                        if 2 * g + n < PAIRS:
                            u = y[:, n * 128 : n * 128 + 128] + eb
                            keep(0, 2 * g + n, u + u * jnp.tanh(u), 0, r, scales[n])

        return mm, finish

    def dilated(ranges, layer, pairs):
        d = 2**layer
        src, dst = layer % 2, 1 - layer % 2
        start, end = ranges[layer + 1]
        begin = max(ranges[layer][0], (start - d) // CHUNK * CHUNK)
        units = chunks(pairs, begin, end)

        def piece(part, step, unit):
            i, r = unit
            ref = low if part else top
            return jnp.concatenate([ref[src, i, r : r + CHUNK], ref[src, i + 1, r : r + CHUNK]], 1)

        def mm(acc):
            multiply(acc, units, piece, ((dil_ref[layer, 0], dil_ref[layer, 1]),))

        def finish(acc):
            for i in pairs:
                near, far = (i, i + 1) if src else (i + 1, i)
                scale = scale_of(layer + 1, i)
                lagged = {}
                for r, y in each(acc, units, i):
                    for k in range(0, CHUNK, 8):
                        lagged[r + k] = y[k : k + 8, 128:]
                        if d < 8:
                            lagged[r + k] = pltpu.roll(lagged[r + k], d, 0)
                    if r < start:
                        continue
                    past = []
                    for k in range(r, r + CHUNK, 8):
                        if d < 8:
                            past.append(jnp.where(sublane < d, lagged.get(k - 8, lagged[k]), lagged[k]))
                        else:
                            past.append(lagged.get(k - d, lagged[k]))
                    u = y[:, :128] + jnp.concatenate(past, 0) + bias[layer + 1 : layer + 2]
                    rows = slice(r, r + CHUNK)
                    h = jnp.where(low_half, hid[src, near, rows], hid[src, far, rows])
                    keep(dst, i, h + u + u * jnp.tanh(u), layer + 1, r, scale)

        return mm, finish

    def decode(ranges, finished):
        units = chunks((0,), *ranges[LAYERS])

        def piece(part, step, unit):
            ref, r = low if part else top, unit[1]
            return jnp.concatenate([ref[0, i, r : r + CHUNK] for i in (2 * step, min(2 * step + 1, 8))], 1)

        def mm(acc):
            multiply(acc, units, piece, [(dec_ref[q],) for q in range(5)])

        def finish(acc):
            for r, y in each(acc, units, 0):
                finished(r, y[:, :128] + y[:, 128:])

        return mm, finish

    tasks = tasks_of(encode, dilated, decode)

    def run(*refs):
        sets = [[refs[(2 * s + n) * SLOTS : (2 * s + n + 1) * SLOTS] for n in range(2)] for s in range(2)]
        waiting, turn = None, 0
        for task in tasks:
            if callable(task):
                task()
                continue
            if task is None:
                if waiting:
                    waiting()
                waiting = None
                continue
            mm, finish = task
            mm(sets[turn])
            if waiting:
                waiting()
            waiting = functools.partial(finish, sets[turn])
            turn = 1 - turn
        if waiting:
            waiting()

    pl.run_scoped(run, *[pltpu.ACC(n)((CHUNK, 256), F32) for s in range(2) for n in range(2) for k in range(SLOTS)])


def all_pairs(layer, group):
    pairs = tuple(range(PAIRS - 1 - layer))
    return [pairs[i : i + group] for i in range(0, len(pairs), group)]


def handed(layer):
    pairs = range(*OWN[layer])
    return list(pairs) if layer == len(OWN) - 1 else [pairs[0], pairs[-1]]


def own(sig_ref, small_ref, dw_ref, enc_ref, *refs):
    outs = refs[: len(OWN)]
    st, hid, top, low, parts, dil_ref = refs[len(OWN) :]
    small = small_ref[...]
    bias = jnp.concatenate([small[18:25], small[18:25]], 1) * 0.5
    st[HIST - 8 : HIST, :] = jnp.zeros((8, 128), F32)
    none = jnp.zeros((EDGE, 2 * HB), F32)
    gather_taps(jnp.concatenate([none, sig_ref[...], none], 0), st, HIST, HH, HB, parts, 1)
    for layer in range(len(OWN) - 1):
        layer_weights(layer, dw_ref, dil_ref)

    def kept(layer, i, value, r):
        if i in handed(layer):
            at = r - LATER[layer][0]
            outs[layer][handed(layer).index(i), at : at + CHUNK] = value

    def tasks(encode, dilated, decode):
        out = [encode(LATER, (g,)) for g in range(OWN[0][0] // 2, OWN[0][1] // 2)]
        for layer in range(len(OWN) - 1):
            pairs = tuple(range(*OWN[layer + 1]))
            out += [dilated(LATER, layer, group) for group in (pairs[:2], *zip(pairs[2:]))]
        return out

    network(tasks, parts, hid, top, low, None, bias, enc_ref, dil_ref, None, kept)


def later(s_ref, small_ref, dw_ref, enc_ref, *refs):
    done = refs[: len(OWN)]
    sums_ref, h4_ref, h5_ref, dil_ref, dec_ref, st, hid, top, low, mask, parts, wide = refs[len(OWN) :]
    small = small_ref[...]
    bias = jnp.concatenate([small[18:25], small[18:25]], 1) * 0.5
    layer_weights(0, dw_ref, dil_ref)
    edge_masks(mask)
    st[HIST - 8 : HIST, :] = jnp.zeros((8, 128), F32)
    gather_taps(s_ref[...], st, HIST, HH, HB, parts, 1)

    def fetch(layer):
        rows = slice(*LATER[layer])
        for k, i in enumerate(handed(layer)):
            value = done[layer][k]
            hid[layer % 2, i, rows] = value
            top[layer % 2, i, rows], low[layer % 2, i, rows] = split(value)

    def kept(layer, i, value, r):
        if layer == 4 and r < EARLIER[5][1]:
            h4_ref[i, r - LATER[4][0] : r - LATER[4][0] + CHUNK] = value
        if layer == 5 and r < EARLIER[6][1]:
            h5_ref[i, r - LATER[5][0] : r - LATER[5][0] + CHUNK] = value

    def store(r, value):
        sums_ref[r - LATER[LAYERS][0] : r - LATER[LAYERS][0] + CHUNK, :] = value

    def tasks(encode, dilated, decode):
        out = [functools.partial(fetch, 0), functools.partial(fetch, 1)]
        out += [encode(LATER, (g,)) for g in range(8) if not OWN[0][0] <= 2 * g < OWN[0][1]]
        for layer in range(LAYERS):
            pairs = [i for i in range(PAIRS - 1 - layer) if layer + 1 >= len(OWN) or i not in range(*OWN[layer + 1])]
            out += [dilated(LATER, layer, pairs[i : i + 2]) for i in range(0, len(pairs), 2)]
            if 2 <= layer + 2 < len(OWN):
                out += [None, functools.partial(fetch, layer + 2)]
            if layer + 1 < LAYERS:
                out.append(functools.partial(layer_weights, layer + 1, dw_ref, dil_ref))
            if layer == 2:
                out.append(lambda: decoder_weights(small[9:18], dec_ref, wide))
        return out + [None, decode(LATER, store)]

    network(tasks, parts, hid, top, low, mask, bias, enc_ref, dil_ref, dec_ref, kept)


def earlier(s_ref, hist_ref, small_ref, enc_ref, sums_ref, h4_ref, h5_ref, dil_ref, dec_ref,
            recon_ref, err_ref, st, hid, top, low, mask, parts, wide, whole):
    small = small_ref[...]
    bias = jnp.concatenate([small[18:25], small[18:25]], 1) * 0.5
    edge_masks(mask)
    hist = jnp.where(lax.axis_index("tm") == 0, 0.0, hist_ref[...])
    gather_taps(jnp.concatenate([hist, s_ref[:, :128]], 1), st, 0, 0, EARLIER[0][1], parts, 8)
    base = EARLIER[LAYERS][0]

    def fetch():
        for buf, ref, begin, end in ((0, h4_ref, 80, 96), (1, h5_ref, 96, 128)):
            for i in range(ref.shape[0]):
                value = ref[i]
                hid[buf, i, begin:end] = value
                top[buf, i, begin:end], low[buf, i, begin:end] = split(value)
        whole[LATER[LAYERS][0] - base :, :] = sums_ref[...]

    def scores(tiles):
        begin, count = HH - base + tiles[0] * TILE_T // 2, len(tiles) * TILE_T // 2
        now, past = whole[begin : begin + count, :], whole[begin - 1 : begin - 1 + count, :]
        wide[pl.ds(tiles[0] * TILE_T, count, 2), :] = now + pltpu.roll(past, 128 - 4 * CB, 1)
        wide[pl.ds(tiles[0] * TILE_T + 1, count, 2), :] = pltpu.roll(now, 128 - 2 * CB, 1)
        for n in tiles:
            cols = slice(n * TILE_T, n * TILE_T + TILE_T)
            out = wide[cols, :].T[: 2 * CB]
            recon_ref[:, cols] = out
            sq = (out - s_ref[EDGE : EDGE + 2 * CB, cols]) ** 2
            per = [jnp.sum(sq[m * TILE_C : m * TILE_C + TILE_C], keepdims=True) for m in range(2 * CB // TILE_C)]
            err_ref[:, n : n + 1] = jnp.concatenate(per, 0) * (1.0 / (TILE_C * TILE_T))

    def store(r, value):
        whole[r - base : r - base + CHUNK, :] = value

    def tasks(encode, dilated, decode):
        out = [encode(EARLIER, (0, 1, 2, 3)), encode(EARLIER, (4, 5, 6, 7)), fetch]
        for layer in range(LAYERS):
            out += [dilated(EARLIER, layer, pairs) for pairs in all_pairs(layer, 4)]
            if layer == 1:
                out.append(functools.partial(scores, (2, 3)))
        return out + [None, decode(EARLIER, store)]

    network(tasks, parts, hid, top, low, mask, bias, enc_ref, dil_ref, dec_ref, lambda layer, i, value, r: None)
    scores((0, 1))


def on_device(signal, encode_weight, encode_bias, dilated_weight, dilated_bias, decode_weight):
    vmem = pl.BlockSpec(memory_space=pltpu.VMEM)
    far = exchange(signal, 1)
    small = jnp.concatenate(
        [encode_weight.T, decode_weight, encode_bias.reshape(1, F), dilated_bias], 0
    )
    near = exchange(signal, 0)
    enc = pl.pallas_call(
        encoder_weights,
        out_shape=jax.ShapeDtypeStruct((8, 2, 256, 256), BF),
        in_specs=[vmem],
        out_specs=vmem,
        scratch_shapes=[pltpu.VMEM((3, 16, 256), F32)],
        cost_estimate=pl.CostEstimate(flops=10**6, bytes_accessed=2 * 10**6, transcendentals=0),
        compiler_params=pltpu.CompilerParams(vmem_limit_bytes=16 * 2**20),
        name="encoder_weights",
    )(small)
    scratch = [
        pltpu.VMEM((HIST + 2 * HB, 128), F32),
        pltpu.VMEM((2, 16, ROWS, 128), F32),
        pltpu.VMEM((2, 16, ROWS, 128), BF),
        pltpu.VMEM((2, 16, ROWS, 128), BF),
    ]
    params = pltpu.CompilerParams(vmem_limit_bytes=32 * 2**20)
    done = pl.pallas_call(
        own,
        out_shape=tuple(jax.ShapeDtypeStruct((len(handed(layer)), HB, 128), F32) for layer in range(len(OWN))),
        in_specs=[vmem] * 4,
        out_specs=(vmem,) * len(OWN),
        scratch_shapes=scratch
        + [pltpu.VMEM((1, 2, ROWS, 256), BF), pltpu.VMEM((len(OWN) - 1, 2, 256, 256), BF)],
        cost_estimate=pl.CostEstimate(flops=10**9, bytes_accessed=2 * 10**6, transcendentals=0),
        compiler_params=params,
        name="own",
    )(signal, small, dilated_weight, enc)
    near, far, *done = lax.optimization_barrier((near, far, *done))
    even = lax.axis_index("fiber") % 2 == 0
    first = lax.axis_index("fiber") == 0
    last = lax.axis_index("fiber") == lax.axis_size("fiber") - 1
    below = jnp.where(first, 0.0, jnp.where(even, far[2 * CB - EDGE :], near[2 * CB - EDGE :]))
    above = jnp.where(last, 0.0, jnp.where(even, near[:EDGE], far[:EDGE]))
    section = jnp.concatenate([below, signal, above], 0)
    history = from_behind(section[:, 2 * HB - HIST :], "tm")
    scratch = scratch + [pltpu.VMEM((LAYERS + 1, 16, 128), F32)]
    results = pl.pallas_call(
        later,
        out_shape=(
            jax.ShapeDtypeStruct((LATER[LAYERS][1] - LATER[LAYERS][0], 128), F32),
            jax.ShapeDtypeStruct((PAIRS - 4, EARLIER[5][1] - LATER[4][0], 128), F32),
            jax.ShapeDtypeStruct((PAIRS - 5, EARLIER[6][1] - LATER[5][0], 128), F32),
            jax.ShapeDtypeStruct((LAYERS, 2, 256, 256), BF),
            jax.ShapeDtypeStruct((5, 256, 256), BF),
        ),
        in_specs=[vmem] * (4 + len(OWN)),
        out_specs=(vmem,) * 5,
        scratch_shapes=scratch + [pltpu.VMEM((1, 2, ROWS, 256), BF), pltpu.VMEM((5, 128, 256), F32)],
        cost_estimate=pl.CostEstimate(flops=7 * 10**9, bytes_accessed=8 * 10**6, transcendentals=0),
        compiler_params=params,
        name="later",
    )(section, small, dilated_weight, enc, *done)
    return pl.pallas_call(
        earlier,
        out_shape=(
            jax.ShapeDtypeStruct((2 * CB, 2 * HB), F32),
            jax.ShapeDtypeStruct((2 * CB // TILE_C, 2 * HB // TILE_T), F32),
        ),
        in_specs=[vmem] * 9,
        out_specs=(vmem,) * 2,
        scratch_shapes=scratch
        + [
            pltpu.VMEM((8, 2, EARLIER[0][1], 256), BF),
            pltpu.VMEM((2 * HB, 128), F32),
            pltpu.VMEM((ROWS - EARLIER[LAYERS][0], 128), F32),
        ],
        cost_estimate=pl.CostEstimate(flops=2 * 10**9, bytes_accessed=8 * 10**6, transcendentals=0),
        compiler_params=params,
        name="earlier",
    )(section, history, small, enc, *results)


def solution(mesh):
    return jax.shard_map(
        on_device,
        mesh=mesh,
        in_specs=(P("fiber", "tm"), P(), P(), P(), P(), P()),
        out_specs=(P("fiber", "tm"), P("fiber", "tm")),
        check_vma=False,
    )
```
